32 devices in a mesh: dp: 8 (over z, y), seq: 4 (over x, core).
Axes of the slice: x: 2, y: 2, z: 4, core: 2. Of those that a mesh axis runs over, the one named last changes fastest.
Arguments:
- queries: bfloat16 [8, 512, 6144], P('dp', 'seq'), may hold values from -6 to 6
- keys: bfloat16 [8, 512, 768], P('dp', 'seq'), may hold values from -6 to 6
- values: bfloat16 [8, 512, 768], P('dp', 'seq'), may hold values from -6 to 6
- segments: int32 [8, 512], P('dp'), may hold values from 0 to 1, never falling along the last dimension, each value on 1 to 384 neighbouring positions
Outputs:
- attended: bfloat16 [8, 512, 6144], P('dp', 'seq')
- query_factor: float32 [48], replicated
- key_head_factor: float32 [6], replicated
The draws below stay inside these ranges and needn't reach their ends.
Inputs may be any that keep to these rules, and one draw needn't show every extreme that they name: `segments`: each row's ids never fall; a document holds at most 384 positions, and some document holds exactly 384.
All inputs are finite; a program needn't handle non-finite values.
Results may differ from the reference program's by a relative error of at most 0.0046.
Values may be sent and summed in bfloat16 or wider, within the bound.
No kernel may reach another device: no remote copies, remote signals or barrier semaphores. Data moves between devices by JAX's collectives and lax.ppermute only.
A program may use at most 64 MiB of HBM per device.

```python
import math
import jax
import jax.numpy as jnp
import numpy as np
from jax import lax

QUERY_HEADS = 48
KEY_VALUE_HEADS = 6
HEAD_SIZE = 128
BATCH_SEQUENCES = 8
PACKED_LENGTH = 512
DOCS = 2
DOCUMENT_LIMIT = 384


def draw_queries(key, part):
    random_seed_key = jax.random.fold_in(key, 11)
    scale_key = jax.random.fold_in(key, 13)
    head_scale = jnp.exp(jax.random.uniform(scale_key, (QUERY_HEADS,), jnp.float32, math.log(0.4), math.log(2.0)))
    noise = jnp.clip(jax.random.normal(random_seed_key, (BATCH_SEQUENCES, PACKED_LENGTH, QUERY_HEADS, HEAD_SIZE), jnp.float32), -3.0, 3.0)
    final_output = noise * head_scale[:, None]
    return final_output.reshape(BATCH_SEQUENCES, PACKED_LENGTH, QUERY_HEADS * HEAD_SIZE).astype(jnp.bfloat16)


def draw_keys(key, part):
    random_seed_key = jax.random.fold_in(key, 17)
    final_output = jnp.clip(jax.random.normal(random_seed_key, (BATCH_SEQUENCES, PACKED_LENGTH, KEY_VALUE_HEADS, HEAD_SIZE), jnp.float32), -3.0, 3.0)
    return final_output.reshape(BATCH_SEQUENCES, PACKED_LENGTH, KEY_VALUE_HEADS * HEAD_SIZE).astype(jnp.bfloat16)


def shard_levels(key, dims, cuts, smallest, top_value):
    factor_of, own = 1.0, jax.random.fold_in(key, 6)
    for dim, shards_of in cuts:
        draws = jnp.exp(jax.random.uniform(jax.random.fold_in(own, dim), (shards_of,), jnp.float32, smallest / len(cuts), top_value / len(cuts)))
        factor_of = factor_of * jnp.repeat(draws, dims[dim] // shards_of).reshape([-1 if axis == dim else 1 for axis in range(len(dims))])
    return factor_of


def length_profile(count, total, bound, skew):
    loads = [(1 << 20) // math.isqrt(standing ** skew) + 1 for standing in range(2, count + 1)]
    surplus, holding = total - bound - (count - 1), [1] * (count - 1)
    while surplus > 0:
        candidates = [i for i in range(count - 1) if holding[i] < bound]
        whole, budget = sum([loads[i] for i in candidates]), surplus
        for i in candidates:
            extra = min(bound - holding[i], max(1, budget * loads[i] // whole), surplus)
            holding[i] = holding[i] + extra
            surplus = surplus - extra
    return np.array([bound] + holding)


def uneven(key, count, total, most, skew):
    if count == 2:
        one = jax.random.randint(key, (), max(1, total - most), min(most, total - 1) + 1)
        return jnp.stack([one, total - one])
    tallies = jnp.asarray(length_profile(count, total, most, skew), jnp.int32)
    couples = (count - 1) // 2
    giver, receiver = tallies[1:1 + 2 * couples:2], tallies[2:2 + 2 * couples:2]
    room = jnp.minimum(giver - 1, most - receiver)
    passed = jax.random.randint(jax.random.fold_in(key, 1), (couples,), 0, 1 << 20) % (room + 1)
    tallies = tallies.at[1:1 + 2 * couples:2].set(giver - passed).at[2:2 + 2 * couples:2].set(receiver + passed)
    return tallies[jax.random.permutation(jax.random.fold_in(key, 2), count)]


def scatter_about(own_key, dims, spread, most, cuts=(), kind=jnp.bfloat16):
    values = spread * jax.random.normal(own_key, dims, jnp.float32)
    if cuts:
        values = values * shard_levels(own_key, dims, cuts, -0.22, 0.18)
    return jnp.clip(values, -most, most).astype(kind)


def setup_inputs(seed: int = 0) -> dict:
    seeds = jax.random.split(jax.random.key(seed), 5)
    queries = draw_queries(jax.random.fold_in(seeds[4], 71), 0)
    keys = draw_keys(jax.random.fold_in(seeds[4], 71), 0)
    values = scatter_about(seeds[2], (BATCH_SEQUENCES, PACKED_LENGTH, KEY_VALUE_HEADS * HEAD_SIZE), 1.0, 6.0, ((0, 8), (1, 4)))
    segments = jax.vmap(lambda own: jnp.searchsorted(jnp.cumsum(uneven(own, DOCS, PACKED_LENGTH, DOCUMENT_LIMIT, 1)), jnp.arange(PACKED_LENGTH), side="right"))(jax.random.split(seeds[3], BATCH_SEQUENCES)).reshape((BATCH_SEQUENCES, PACKED_LENGTH)).astype(jnp.int32)
    return {"queries": queries, "keys": keys, "values": values, "segments": segments}


clip_level = 6.0

def attend(query_block, key_block, value_block, query_pos, key_pos, doc_ids):
    scale = query_block.shape[-1] ** (-0.5)
    logits = jnp.einsum('qcgd,kcd->cgqk', query_block.astype(jnp.float32), key_block.astype(jnp.float32)) * scale
    query_doc = jnp.take(doc_ids, query_pos)
    key_doc = jnp.take(doc_ids, jnp.maximum(key_pos, 0))
    valid = (key_pos[None, :] <= query_pos[:, None]) & (key_pos[None, :] >= 0) & (key_doc[None, :] == query_doc[:, None])
    logits = jnp.where(valid, logits, -1e+30)
    largest = lax.optimization_barrier(jnp.max(logits, axis=-1, keepdims=True))
    expo = jnp.exp(logits - largest)
    total = lax.optimization_barrier(jnp.sum(expo, axis=-1, keepdims=True))
    weights = (expo / total).astype(jnp.bfloat16)
    mixed = jnp.einsum('cgqk,kcd->qcgd', weights.astype(jnp.float32), value_block.astype(jnp.float32)).astype(jnp.bfloat16)
    return (mixed, lax.optimization_barrier(jnp.max(largest[..., 0], axis=-1)))

def clip_factors(head_max):
    query_group = QUERY_HEADS // KEY_VALUE_HEADS
    clipped_logits = clip_level / jnp.maximum(head_max, clip_level)
    key_head_factor = jnp.sqrt(lax.optimization_barrier(jnp.min(clipped_logits.reshape(KEY_VALUE_HEADS, query_group), axis=1)))
    query_factor = clipped_logits / jnp.repeat(key_head_factor, query_group)
    return (query_factor, key_head_factor)

def reference(queries, keys, values, segments):
    query_group = QUERY_HEADS // KEY_VALUE_HEADS
    block = min(512, PACKED_LENGTH)
    blocks = PACKED_LENGTH // block

    def one_row(items):
        query_row_vector, key_row_vector, value_row_vector, doc_ids = items
        query_head_list = query_row_vector.reshape(PACKED_LENGTH, KEY_VALUE_HEADS, query_group, HEAD_SIZE)
        leading_part = jnp.zeros((DOCUMENT_LIMIT, KEY_VALUE_HEADS, HEAD_SIZE), jnp.bfloat16)
        key_padding = jnp.concatenate([leading_part, key_row_vector.reshape(PACKED_LENGTH, KEY_VALUE_HEADS, HEAD_SIZE)], axis=0)
        value_padding = jnp.concatenate([leading_part, value_row_vector.reshape(PACKED_LENGTH, KEY_VALUE_HEADS, HEAD_SIZE)], axis=0)
        pieces = []
        maxima = []
        for number in range(blocks):
            start = number * block
            query_pos = jnp.arange(block, dtype=jnp.int32) + start
            key_pos = jnp.arange(block + DOCUMENT_LIMIT, dtype=jnp.int32) + (start - DOCUMENT_LIMIT)
            mixed, largest = attend(query_head_list[start:start + block], key_padding[start:start + block + DOCUMENT_LIMIT], value_padding[start:start + block + DOCUMENT_LIMIT], query_pos, key_pos, doc_ids)
            pieces.append(mixed.reshape(block, QUERY_HEADS * HEAD_SIZE))
            maxima.append(largest.reshape(QUERY_HEADS))
        return (jnp.concatenate(pieces, axis=0), lax.optimization_barrier(jnp.max(jnp.stack(maxima), axis=0)))
    attended, row_max = lax.map(one_row, (queries, keys, values, segments))
    query_factor, key_head_factor = clip_factors(lax.optimization_barrier(jnp.max(row_max, axis=0)))
    return (attended, query_factor, key_head_factor)
```

```python
import functools
import math

import jax
import jax.numpy as jnp
from jax import lax
from jax.experimental import pallas as pl
from jax.experimental.pallas import tpu as pltpu
from jax.sharding import PartitionSpec as P

QUERY_HEADS = 48
KEY_VALUE_HEADS = 6
HEAD_SIZE = 128
DOCUMENT_LIMIT = 384
GROUP = QUERY_HEADS // KEY_VALUE_HEADS

clip_level = 6.0
SCALE = HEAD_SIZE ** (-0.5)
SCALE_2 = SCALE * math.log2(math.e)
MASKED = -1e30
NT = (((1,), (1,)), ((), ()))


def reach_of(rows, length, shards):
    reach = (DOCUMENT_LIMIT - 1 + rows - 1) // rows
    documents = length // 256
    least = length - (documents - 1) * DOCUMENT_LIMIT
    if shards == reach + 1 and documents > 1 and least >= rows:
        reach -= 1
    return reach


def fill_bias(seg_ref, bias_ref, rank, reach, rows):
    own = seg_ref[:, pl.ds(pl.multiple_of(rank * rows, rows), rows)]
    query_doc = jnp.broadcast_to(own, (rows, rows))
    key_index = lax.broadcasted_iota(jnp.int32, (rows, rows), 0)
    query_index = lax.broadcasted_iota(jnp.int32, (rows, rows), 1)
    for distance in range(reach + 1):
        block = jnp.maximum(rank - distance, 0)
        docs = seg_ref[:, pl.ds(pl.multiple_of(block * rows, rows), rows)]
        key_doc = jnp.broadcast_to(docs, (rows, rows)).T
        valid = key_doc == query_doc
        if distance == 0:
            valid = valid & (key_index <= query_index)
        else:
            valid = valid & (rank >= distance)
        bias_ref[distance * rows : (distance + 1) * rows, :] = jnp.where(valid, 0.0, MASKED)


def max_kernel(reach, shards_all, rank_ref, seg_ref, q_ref, *refs):
    key_refs, (row_max_ref, head_max_ref, bias_ref) = refs[: reach + 1], refs[reach + 1 :]
    rows = q_ref.shape[0]
    fill_bias(seg_ref, bias_ref, rank_ref[0], reach, rows)
    for column in range(KEY_VALUE_HEADS):
        at = slice(column * HEAD_SIZE, (column + 1) * HEAD_SIZE)
        key_block = jnp.concatenate([k[:, at] for k in key_refs], axis=0)
        for head in range(column * GROUP, (column + 1) * GROUP):
            q = q_ref[:, head * HEAD_SIZE : (head + 1) * HEAD_SIZE]
            logits = lax.dot_general(key_block, q, NT, preferred_element_type=jnp.float32)
            row_max_ref[head : head + 1, :] = jnp.max(
                logits + bias_ref[...], axis=0, keepdims=True
            )
    largest = row_max_ref[...]
    padded = jnp.concatenate([largest, largest, largest], axis=0)[:rows]
    head_max = jnp.max(padded.T, axis=0, keepdims=True) * SCALE
    head_max_ref[...] = jnp.broadcast_to(head_max[None], head_max_ref.shape)


def mix_kernel(reach, rank_ref, seg_ref, q_ref, row_max_ref, *refs):
    key_refs, value_refs = refs[: reach + 1], refs[reach + 1 : 2 * reach + 2]
    out_ref, bias_ref = refs[2 * reach + 2 :]
    rows = q_ref.shape[0]
    fill_bias(seg_ref, bias_ref, rank_ref[0], reach, rows)
    ones = jnp.ones((16, (reach + 1) * rows), jnp.bfloat16)
    for column in range(KEY_VALUE_HEADS):
        at = slice(column * HEAD_SIZE, (column + 1) * HEAD_SIZE)
        key_block = jnp.concatenate([k[:, at] for k in key_refs], axis=0)
        value_block = jnp.concatenate([v[:, at].T for v in value_refs], axis=1)
        value_block = jnp.concatenate([value_block, ones], axis=0)
        for head in range(column * GROUP, (column + 1) * GROUP):
            here = slice(head * HEAD_SIZE, (head + 1) * HEAD_SIZE)
            logits = lax.dot_general(
                key_block, q_ref[:, here], NT, preferred_element_type=jnp.float32
            )
            largest = row_max_ref[head : head + 1, :] * SCALE_2
            expo = jnp.exp2((logits + bias_ref[...]) * SCALE_2 - largest).astype(jnp.bfloat16)
            mixed = jnp.dot(value_block, expo, preferred_element_type=jnp.float32)
            share = 1.0 / mixed[HEAD_SIZE : HEAD_SIZE + 1, :]
            mixed = (mixed[:HEAD_SIZE, :] * share).astype(jnp.bfloat16)
            out_ref[:, here] = mixed.T


def row_maxima(rank, segments, queries, key_blocks, devices):
    reach, rows = len(key_blocks) - 1, queries.shape[0]
    vmem = pl.BlockSpec(memory_space=pltpu.VMEM)
    return pl.pallas_call(
        functools.partial(max_kernel, reach, devices),
        out_shape=(
            jax.ShapeDtypeStruct((QUERY_HEADS, rows), jnp.float32),
            jax.ShapeDtypeStruct((devices, 1, rows), jnp.float32),
        ),
        in_specs=[pl.BlockSpec(memory_space=pltpu.SMEM)] + [vmem] * (reach + 3),
        out_specs=(vmem, vmem),
        scratch_shapes=[pltpu.VMEM(((reach + 1) * rows, rows), jnp.float32)],
        compiler_params=pltpu.CompilerParams(vmem_limit_bytes=24 << 20),
        cost_estimate=pl.CostEstimate(
            flops=2 * QUERY_HEADS * HEAD_SIZE * rows * rows * (reach + 1),
            bytes_accessed=2 * queries.size,
            transcendentals=0,
        ),
        name="row_maxima",
    )(rank, segments, queries, *key_blocks)


def mix(rank, segments, queries, row_max, key_blocks, value_blocks):
    reach, rows = len(key_blocks) - 1, queries.shape[0]
    vmem = pl.BlockSpec(memory_space=pltpu.VMEM)
    return pl.pallas_call(
        functools.partial(mix_kernel, reach),
        out_shape=jax.ShapeDtypeStruct(queries.shape, jnp.bfloat16),
        in_specs=[pl.BlockSpec(memory_space=pltpu.SMEM)] + [vmem] * (2 * reach + 5),
        out_specs=vmem,
        scratch_shapes=[pltpu.VMEM(((reach + 1) * rows, rows), jnp.float32)],
        compiler_params=pltpu.CompilerParams(vmem_limit_bytes=24 << 20),
        cost_estimate=pl.CostEstimate(
            flops=4 * QUERY_HEADS * HEAD_SIZE * rows * rows * (reach + 1),
            bytes_accessed=4 * queries.size,
            transcendentals=QUERY_HEADS * rows * rows * (reach + 1),
        ),
        name="mix",
    )(rank, segments, queries, row_max, *key_blocks, *value_blocks)


def passed_along(x, by):
    shards = lax.axis_size("seq")
    pairs = [(i, i + by) for i in range(shards - by)]
    return lax.ppermute(x, "seq", pairs)


def clip_factors(head_max):
    clipped_logits = clip_level / jnp.maximum(head_max, clip_level)
    key_head_factor = jnp.sqrt(jnp.min(clipped_logits.reshape(KEY_VALUE_HEADS, GROUP), axis=1))
    query_factor = clipped_logits / jnp.repeat(key_head_factor, GROUP)
    return (query_factor, key_head_factor)


def local(queries, keys, values, segments):
    rows, length = queries.shape[1], segments.shape[1]
    shards = lax.axis_size("seq")
    devices = lax.axis_size("dp") * shards
    reach = reach_of(rows, length, shards)
    rank = lax.axis_index("seq").astype(jnp.int32).reshape(1)
    queries, keys, values = queries[0], keys[0], values[0]

    key_blocks = [keys] + [passed_along(keys, d) for d in range(1, reach + 1)]
    value_blocks = [values] + [passed_along(values, d) for d in range(1, reach + 1)]
    row_max, head_max = row_maxima(rank, segments, queries, key_blocks, devices)
    everyone = lax.all_to_all(head_max, ("dp", "seq"), 0, 0)
    attended = mix(rank, segments, queries, row_max, key_blocks, value_blocks)
    query_factor, key_head_factor = clip_factors(
        jnp.max(everyone[:, 0, :QUERY_HEADS], axis=0)
    )
    return (attended[None], query_factor, key_head_factor)


def solution(mesh):
    in_specs = (P("dp", "seq", None), P("dp", "seq", None), P("dp", "seq", None), P("dp", None))
    out_specs = (P("dp", "seq", None), P(), P())
    return jax.shard_map(local, mesh=mesh, in_specs=in_specs, out_specs=out_specs, check_vma=False)
```

```python
import functools
import math

import jax
import jax.numpy as jnp
from jax import lax
from jax.experimental import pallas as pl
from jax.experimental.pallas import tpu as pltpu
from jax.sharding import PartitionSpec as P

QUERY_HEADS = 48
KEY_VALUE_HEADS = 6
HEAD_SIZE = 128
DOCUMENT_LIMIT = 384
GROUP = QUERY_HEADS // KEY_VALUE_HEADS

clip_level = 6.0
SCALE = HEAD_SIZE ** (-0.5)
SCALE_2 = SCALE * math.log2(math.e)
MASKED = -1e30
NT = (((1,), (1,)), ((), ()))


def reach_of(rows, length, shards):
    reach = (DOCUMENT_LIMIT - 1 + rows - 1) // rows
    documents = length // 256
    least = length - (documents - 1) * DOCUMENT_LIMIT
    if shards == reach + 1 and documents > 1 and least >= rows:
        reach -= 1
    return reach


def fill_bias(seg_ref, bias_ref, rank, distances, rows):
    own = seg_ref[:, pl.ds(pl.multiple_of(rank * rows, rows), rows)]
    query_doc = jnp.broadcast_to(own, (rows, rows))
    key_index = lax.broadcasted_iota(jnp.int32, (rows, rows), 0)
    query_index = lax.broadcasted_iota(jnp.int32, (rows, rows), 1)
    for place, distance in enumerate(distances):
        block = jnp.maximum(rank - distance, 0)
        docs = seg_ref[:, pl.ds(pl.multiple_of(block * rows, rows), rows)]
        key_doc = jnp.broadcast_to(docs, (rows, rows)).T
        valid = key_doc == query_doc
        if distance == 0:
            valid = valid & (key_index <= query_index)
        else:
            valid = valid & (rank >= distance)
        bias_ref[place * rows : (place + 1) * rows, :] = jnp.where(valid, 0.0, MASKED)


def block_maxima(q_ref, key_refs, bias_ref, head):
    column = head // GROUP
    at = slice(column * HEAD_SIZE, (column + 1) * HEAD_SIZE)
    key_block = jnp.concatenate([k[:, at] for k in key_refs], axis=0)
    q = q_ref[:, head * HEAD_SIZE : (head + 1) * HEAD_SIZE]
    logits = lax.dot_general(key_block, q, NT, preferred_element_type=jnp.float32)
    return jnp.max(logits + bias_ref[...], axis=0, keepdims=True)


def own_max_kernel(rank_ref, seg_ref, q_ref, key_ref, own_max_ref, bias_ref):
    fill_bias(seg_ref, bias_ref, rank_ref[0], (0,), q_ref.shape[0])
    for head in range(QUERY_HEADS):
        own_max_ref[head : head + 1, :] = block_maxima(q_ref, (key_ref,), bias_ref, head)


def max_kernel(reach, rank_ref, seg_ref, q_ref, own_max_ref, *refs):
    key_refs, (row_max_ref, head_max_ref, bias_ref) = refs[:reach], refs[reach:]
    rows = q_ref.shape[0]
    fill_bias(seg_ref, bias_ref, rank_ref[0], range(1, reach + 1), rows)
    for head in range(QUERY_HEADS):
        row_max_ref[head : head + 1, :] = jnp.maximum(
            own_max_ref[head : head + 1, :], block_maxima(q_ref, key_refs, bias_ref, head)
        )
    largest = row_max_ref[...]
    padded = jnp.concatenate([largest, largest, largest], axis=0)[:rows]
    head_max = jnp.max(padded.T, axis=0, keepdims=True) * SCALE
    head_max_ref[...] = jnp.broadcast_to(head_max[None], head_max_ref.shape)


def mix_kernel(reach, rank_ref, seg_ref, q_ref, row_max_ref, *refs):
    key_refs, value_refs = refs[: reach + 1], refs[reach + 1 : 2 * reach + 2]
    out_ref, bias_ref = refs[2 * reach + 2 :]
    rows = q_ref.shape[0]
    fill_bias(seg_ref, bias_ref, rank_ref[0], range(reach + 1), rows)
    for column in range(KEY_VALUE_HEADS):
        at = slice(column * HEAD_SIZE, (column + 1) * HEAD_SIZE)
        key_block = jnp.concatenate([k[:, at] for k in key_refs], axis=0)
        value_block = jnp.concatenate([v[:, at].T for v in value_refs], axis=1)
        for head in range(column * GROUP, (column + 1) * GROUP):
            here = slice(head * HEAD_SIZE, (head + 1) * HEAD_SIZE)
            logits = lax.dot_general(
                key_block, q_ref[:, here], NT, preferred_element_type=jnp.float32
            )
            largest = row_max_ref[head : head + 1, :] * SCALE_2
            expo = jnp.exp2((logits + bias_ref[...]) * SCALE_2 - largest)
            share = 1.0 / jnp.sum(expo, axis=0, keepdims=True)
            mixed = jnp.dot(
                value_block, expo.astype(jnp.bfloat16), preferred_element_type=jnp.float32
            )
            out_ref[:, here] = (mixed * share).astype(jnp.bfloat16).T


VMEM = pl.BlockSpec(memory_space=pltpu.VMEM)


def call(kernel, name, out_shape, blocks, rows, products, exponentials, rank, *arrays):
    several = isinstance(out_shape, tuple)
    pairs = QUERY_HEADS * rows * rows * blocks
    return pl.pallas_call(
        kernel,
        out_shape=out_shape,
        in_specs=[pl.BlockSpec(memory_space=pltpu.SMEM)] + [VMEM] * len(arrays),
        out_specs=(VMEM,) * len(out_shape) if several else VMEM,
        scratch_shapes=[pltpu.VMEM((blocks * rows, rows), jnp.float32)],
        compiler_params=pltpu.CompilerParams(vmem_limit_bytes=24 << 20),
        cost_estimate=pl.CostEstimate(
            flops=2 * products * HEAD_SIZE * pairs,
            bytes_accessed=2 * QUERY_HEADS * HEAD_SIZE * rows * products,
            transcendentals=exponentials * pairs,
        ),
        name=name,
    )(rank, *arrays)


def own_maxima(rank, segments, queries, keys):
    rows = queries.shape[0]
    out_shape = jax.ShapeDtypeStruct((QUERY_HEADS, rows), jnp.float32)
    return call(
        own_max_kernel, "own_maxima", out_shape, 1, rows, 1, 0, rank, segments, queries, keys
    )


def row_maxima(rank, segments, queries, own_max, key_blocks, devices):
    reach, rows = len(key_blocks), queries.shape[0]
    out_shape = (
        jax.ShapeDtypeStruct((QUERY_HEADS, rows), jnp.float32),
        jax.ShapeDtypeStruct((devices, 1, rows), jnp.float32),
    )
    kernel = functools.partial(max_kernel, reach)
    return call(
        kernel, "row_maxima", out_shape, reach, rows, 1, 0, rank, segments, queries, own_max, *key_blocks
    )


def mix(rank, segments, queries, row_max, key_blocks, value_blocks):
    reach, rows = len(key_blocks) - 1, queries.shape[0]
    out_shape = jax.ShapeDtypeStruct(queries.shape, jnp.bfloat16)
    kernel = functools.partial(mix_kernel, reach)
    arrays = (rank, segments, queries, row_max, *key_blocks, *value_blocks)
    return call(kernel, "mix", out_shape, reach + 1, rows, 2, 1, *arrays)


def passed_along(x, by):
    shards = lax.axis_size("seq")
    pairs = [(i, i + by) for i in range(shards - by)]
    return lax.ppermute(x, "seq", pairs)


def clip_factors(head_max):
    clipped_logits = clip_level / jnp.maximum(head_max, clip_level)
    key_head_factor = jnp.sqrt(jnp.min(clipped_logits.reshape(KEY_VALUE_HEADS, GROUP), axis=1))
    query_factor = clipped_logits / jnp.repeat(key_head_factor, GROUP)
    return (query_factor, key_head_factor)


def local(queries, keys, values, segments):
    rows, length = queries.shape[1], segments.shape[1]
    shards = lax.axis_size("seq")
    devices = lax.axis_size("dp") * shards
    reach = reach_of(rows, length, shards)
    rank = lax.axis_index("seq").astype(jnp.int32).reshape(1)
    queries, keys, values = queries[0], keys[0], values[0]

    earlier_keys = [passed_along(keys, d) for d in range(1, reach + 1)]
    own_max = own_maxima(rank, segments, queries, keys)
    sent_values, own_max = lax.optimization_barrier((values, own_max))
    earlier_values = [passed_along(sent_values, d) for d in range(1, reach + 1)]
    row_max, head_max = row_maxima(rank, segments, queries, own_max, earlier_keys, devices)
    everyone = lax.all_to_all(head_max, ("dp", "seq"), 0, 0)
    attended = mix(
        rank, segments, queries, row_max, [keys] + earlier_keys, [values] + earlier_values
    )
    query_factor, key_head_factor = clip_factors(
        jnp.max(everyone[:, 0, :QUERY_HEADS], axis=0)
    )
    return (attended[None], query_factor, key_head_factor)


def solution(mesh):
    in_specs = (P("dp", "seq", None), P("dp", "seq", None), P("dp", "seq", None), P("dp", None))
    out_specs = (P("dp", "seq", None), P(), P())
    return jax.shard_map(local, mesh=mesh, in_specs=in_specs, out_specs=out_specs, check_vma=False)
```

```python
import functools
import math

import jax
import jax.numpy as jnp
from jax import lax
from jax.experimental import pallas as pl
from jax.experimental.pallas import tpu as pltpu
from jax.sharding import PartitionSpec as P

QUERY_HEADS = 48
KEY_VALUE_HEADS = 6
HEAD_SIZE = 128
DOCUMENT_LIMIT = 384
GROUP = QUERY_HEADS // KEY_VALUE_HEADS

clip_level = 6.0
SCALE = HEAD_SIZE ** (-0.5)
SCALE_2 = SCALE * math.log2(math.e)
MASKED = -1e30
NT = (((1,), (1,)), ((), ()))


def reach_of(rows, length, shards):
    reach = (DOCUMENT_LIMIT - 1 + rows - 1) // rows
    documents = length // 256
    least = length - (documents - 1) * DOCUMENT_LIMIT
    if shards == reach + 1 and documents > 1 and least >= rows:
        reach -= 1
    return reach


def fill_bias(seg_ref, bias_ref, rank, distances, rows):
    own = seg_ref[:, pl.ds(pl.multiple_of(rank * rows, rows), rows)]
    query_doc = jnp.broadcast_to(own, (rows, rows))
    key_index = lax.broadcasted_iota(jnp.int32, (rows, rows), 0)
    query_index = lax.broadcasted_iota(jnp.int32, (rows, rows), 1)
    for place, distance in enumerate(distances):
        block = jnp.maximum(rank - distance, 0)
        docs = seg_ref[:, pl.ds(pl.multiple_of(block * rows, rows), rows)]
        key_doc = jnp.broadcast_to(docs, (rows, rows)).T
        valid = key_doc == query_doc
        if distance == 0:
            valid = valid & (key_index <= query_index)
        else:
            valid = valid & (rank >= distance)
        bias_ref[place * rows : (place + 1) * rows, :] = jnp.where(valid, 0.0, MASKED)


def block_maxima(q_ref, key_refs, bias_ref, head):
    column = head // GROUP
    at = slice(column * HEAD_SIZE, (column + 1) * HEAD_SIZE)
    key_block = jnp.concatenate([k[:, at] for k in key_refs], axis=0)
    q = q_ref[:, head * HEAD_SIZE : (head + 1) * HEAD_SIZE]
    logits = lax.dot_general(key_block, q, NT, preferred_element_type=jnp.float32)
    return jnp.max(logits + bias_ref[...], axis=0, keepdims=True)


def own_max_kernel(rank_ref, seg_ref, q_ref, key_ref, own_max_ref, bias_ref):
    fill_bias(seg_ref, bias_ref, rank_ref[0], (0,), q_ref.shape[0])
    for head in range(QUERY_HEADS):
        own_max_ref[head : head + 1, :] = block_maxima(q_ref, (key_ref,), bias_ref, head)


def max_kernel(reach, rank_ref, seg_ref, q_ref, own_max_ref, *refs):
    key_refs, (row_max_ref, head_max_ref, bias_ref) = refs[:reach], refs[reach:]
    rows = q_ref.shape[0]
    fill_bias(seg_ref, bias_ref, rank_ref[0], range(1, reach + 1), rows)
    for head in range(QUERY_HEADS):
        row_max_ref[head : head + 1, :] = jnp.maximum(
            own_max_ref[head : head + 1, :], block_maxima(q_ref, key_refs, bias_ref, head)
        )
    largest = row_max_ref[...]
    padded = jnp.concatenate([largest, largest, largest], axis=0)[:rows]
    head_max = jnp.max(padded.T, axis=0, keepdims=True) * SCALE
    head_max_ref[...] = jnp.broadcast_to(head_max[None], head_max_ref.shape)


def mix_kernel(reach, rank_ref, seg_ref, q_ref, row_max_ref, *refs):
    key_refs, value_refs = refs[: reach + 1], refs[reach + 1 : 2 * reach + 2]
    out_ref, bias_ref = refs[2 * reach + 2 :]
    rows = q_ref.shape[0]
    fill_bias(seg_ref, bias_ref, rank_ref[0], range(reach + 1), rows)
    for column in range(KEY_VALUE_HEADS):
        at = slice(column * HEAD_SIZE, (column + 1) * HEAD_SIZE)
        key_block = jnp.concatenate([k[:, at] for k in key_refs], axis=0)
        value_block = jnp.concatenate([v[:, at].T for v in value_refs], axis=1)
        for head in range(column * GROUP, (column + 1) * GROUP):
            here = slice(head * HEAD_SIZE, (head + 1) * HEAD_SIZE)
            logits = lax.dot_general(
                key_block, q_ref[:, here], NT, preferred_element_type=jnp.float32
            )
            largest = row_max_ref[head : head + 1, :] * SCALE_2
            expo = jnp.exp2((logits + bias_ref[...]) * SCALE_2 - largest)
            share = 1.0 / jnp.sum(expo, axis=0, keepdims=True)
            mixed = jnp.dot(
                value_block, expo.astype(jnp.bfloat16), preferred_element_type=jnp.float32
            )
            out_ref[:, here] = (mixed * share).astype(jnp.bfloat16).T


VMEM = pl.BlockSpec(memory_space=pltpu.VMEM)


def call(kernel, name, out_shape, blocks, rows, products, exponentials, rank, *arrays):
    several = isinstance(out_shape, tuple)
    pairs = QUERY_HEADS * rows * rows * blocks
    return pl.pallas_call(
        kernel,
        out_shape=out_shape,
        in_specs=[pl.BlockSpec(memory_space=pltpu.SMEM)] + [VMEM] * len(arrays),
        out_specs=(VMEM,) * len(out_shape) if several else VMEM,
        scratch_shapes=[pltpu.VMEM((blocks * rows, rows), jnp.float32)],
        compiler_params=pltpu.CompilerParams(vmem_limit_bytes=24 << 20),
        cost_estimate=pl.CostEstimate(
            flops=2 * products * HEAD_SIZE * pairs,
            bytes_accessed=2 * QUERY_HEADS * HEAD_SIZE * rows * products,
            transcendentals=exponentials * pairs,
        ),
        name=name,
    )(rank, *arrays)


def own_maxima(rank, segments, queries, keys):
    rows = queries.shape[0]
    out_shape = jax.ShapeDtypeStruct((QUERY_HEADS, rows), jnp.float32)
    return call(
        own_max_kernel, "own_maxima", out_shape, 1, rows, 1, 0, rank, segments, queries, keys
    )


def row_maxima(rank, segments, queries, own_max, key_blocks, devices):
    reach, rows = len(key_blocks), queries.shape[0]
    out_shape = (
        jax.ShapeDtypeStruct((QUERY_HEADS, rows), jnp.float32),
        jax.ShapeDtypeStruct((devices, 1, rows), jnp.float32),
    )
    kernel = functools.partial(max_kernel, reach)
    return call(
        kernel, "row_maxima", out_shape, reach, rows, 1, 0, rank, segments, queries, own_max, *key_blocks
    )


def mix(rank, segments, queries, row_max, key_blocks, value_blocks):
    reach, rows = len(key_blocks) - 1, queries.shape[0]
    out_shape = jax.ShapeDtypeStruct(queries.shape, jnp.bfloat16)
    kernel = functools.partial(mix_kernel, reach)
    arrays = (rank, segments, queries, row_max, *key_blocks, *value_blocks)
    return call(kernel, "mix", out_shape, reach + 1, rows, 2, 1, *arrays)


def passed_along(x, by):
    shards = lax.axis_size("seq")
    return lax.ppermute(x, "seq", [(i, (i + by) % shards) for i in range(shards)])


def clip_factors(head_max):
    clipped_logits = clip_level / jnp.maximum(head_max, clip_level)
    key_head_factor = jnp.sqrt(jnp.min(clipped_logits.reshape(KEY_VALUE_HEADS, GROUP), axis=1))
    query_factor = clipped_logits / jnp.repeat(key_head_factor, GROUP)
    return (query_factor, key_head_factor)


def local(queries, keys, values, segments):
    rows, length = queries.shape[1], segments.shape[1]
    shards = lax.axis_size("seq")
    devices = lax.axis_size("dp") * shards
    reach = reach_of(rows, length, shards)
    rank = lax.axis_index("seq").astype(jnp.int32).reshape(1)
    queries, keys, values = queries[0], keys[0], values[0]

    earlier_keys = [passed_along(keys, d) for d in range(reach, 0, -1)][::-1]
    own_max = own_maxima(rank, segments, queries, keys)
    sent_values, own_max = lax.optimization_barrier((values, own_max))
    earlier_values = [passed_along(sent_values, d) for d in range(reach, 0, -1)][::-1]
    row_max, head_max = row_maxima(rank, segments, queries, own_max, earlier_keys, devices)
    everyone = lax.all_to_all(head_max, ("dp", "seq"), 0, 0)
    attended = mix(
        rank, segments, queries, row_max, [keys] + earlier_keys, [values] + earlier_values
    )
    query_factor, key_head_factor = clip_factors(
        jnp.max(everyone[:, 0, :QUERY_HEADS], axis=0)
    )
    return (attended[None], query_factor, key_head_factor)


def solution(mesh):
    in_specs = (P("dp", "seq", None), P("dp", "seq", None), P("dp", "seq", None), P("dp", None))
    out_specs = (P("dp", "seq", None), P(), P())
    return jax.shard_map(local, mesh=mesh, in_specs=in_specs, out_specs=out_specs, check_vma=False)
```

```python
import functools
import math

import jax
import jax.numpy as jnp
from jax import lax
from jax.experimental import pallas as pl
from jax.experimental.pallas import tpu as pltpu
from jax.sharding import PartitionSpec as P

QUERY_HEADS = 48
KEY_VALUE_HEADS = 6
HEAD_SIZE = 128
DOCUMENT_LIMIT = 384
GROUP = QUERY_HEADS // KEY_VALUE_HEADS

clip_level = 6.0
SCALE = HEAD_SIZE ** (-0.5)
SCALE_2 = SCALE * math.log2(math.e)
MASKED = -1e30
NT = (((1,), (1,)), ((), ()))


def reach_of(rows, length, shards):
    reach = (DOCUMENT_LIMIT - 1 + rows - 1) // rows
    documents = length // 256
    least = length - (documents - 1) * DOCUMENT_LIMIT
    if shards == reach + 1 and documents > 1 and least >= rows:
        reach -= 1
    return reach


def fill_bias(seg_ref, bias_ref, rank, reach, rows):
    own = seg_ref[:, pl.ds(pl.multiple_of(rank * rows, rows), rows)]
    query_doc = jnp.broadcast_to(own, (rows, rows))
    key_index = lax.broadcasted_iota(jnp.int32, (rows, rows), 0)
    query_index = lax.broadcasted_iota(jnp.int32, (rows, rows), 1)
    for distance in range(reach + 1):
        block = jnp.maximum(rank - distance, 0)
        docs = seg_ref[:, pl.ds(pl.multiple_of(block * rows, rows), rows)]
        key_doc = jnp.broadcast_to(docs, (rows, rows)).T
        valid = key_doc == query_doc
        if distance == 0:
            valid = valid & (key_index <= query_index)
        else:
            valid = valid & (rank >= distance)
        bias_ref[distance * rows : (distance + 1) * rows, :] = jnp.where(valid, 0.0, MASKED)


def block_maxima(q_ref, key_ref, bias_ref, distance, head):
    rows = q_ref.shape[0]
    column = head // GROUP
    keys = key_ref[:, column * HEAD_SIZE : (column + 1) * HEAD_SIZE]
    q = [q_ref[:, h * HEAD_SIZE : (h + 1) * HEAD_SIZE] for h in (head, head + 1)]
    logits = lax.dot_general(
        keys, jnp.concatenate(q, axis=0), NT, preferred_element_type=jnp.float32
    )
    bias = bias_ref[distance * rows : (distance + 1) * rows, :]
    return [
        jnp.max(logits[:, i * rows : (i + 1) * rows] + bias, axis=0, keepdims=True)
        for i in range(2)
    ]


def own_max_kernel(reach, rank_ref, seg_ref, q_ref, key_ref, own_max_ref, bias_ref):
    fill_bias(seg_ref, bias_ref, rank_ref[0], reach, q_ref.shape[0])
    for head in range(0, QUERY_HEADS, 2):
        first, second = block_maxima(q_ref, key_ref, bias_ref, 0, head)
        own_max_ref[head : head + 1, :] = first
        own_max_ref[head + 1 : head + 2, :] = second


def next_max_kernel(distance, bias_ref, q_ref, max_ref, key_ref, row_max_ref, *head_max_refs):
    rows = q_ref.shape[0]
    for head in range(0, QUERY_HEADS, 2):
        for i, largest in enumerate(block_maxima(q_ref, key_ref, bias_ref, distance, head)):
            at = slice(head + i, head + i + 1)
            row_max_ref[at, :] = jnp.maximum(max_ref[at, :], largest)
    for head_max_ref in head_max_refs:
        largest = row_max_ref[...]
        padded = jnp.concatenate([largest, largest, largest], axis=0)[:rows]
        head_max = jnp.max(padded.T, axis=0, keepdims=True) * SCALE
        head_max_ref[...] = jnp.broadcast_to(head_max[None], head_max_ref.shape)


def mix_kernel(reach, bias_ref, q_ref, row_max_ref, *refs):
    key_refs, value_refs, out_ref = refs[: reach + 1], refs[reach + 1 : 2 * reach + 2], refs[-1]
    for column in range(KEY_VALUE_HEADS):
        at = slice(column * HEAD_SIZE, (column + 1) * HEAD_SIZE)
        key_block = jnp.concatenate([k[:, at] for k in key_refs], axis=0)
        value_block = jnp.concatenate([v[:, at].T for v in value_refs], axis=1)
        for head in range(column * GROUP, (column + 1) * GROUP):
            here = slice(head * HEAD_SIZE, (head + 1) * HEAD_SIZE)
            logits = lax.dot_general(
                key_block, q_ref[:, here], NT, preferred_element_type=jnp.float32
            )
            largest = row_max_ref[head : head + 1, :] * SCALE_2
            expo = jnp.exp2((logits + bias_ref[...]) * SCALE_2 - largest)
            share = 1.0 / jnp.sum(expo, axis=0, keepdims=True)
            mixed = jnp.dot(
                value_block, expo.astype(jnp.bfloat16), preferred_element_type=jnp.float32
            )
            out_ref[:, here] = (mixed * share).astype(jnp.bfloat16).T


VMEM = pl.BlockSpec(memory_space=pltpu.VMEM)


def call(kernel, name, out_shape, blocks, rows, products, *arrays, scalars=0):
    pairs = QUERY_HEADS * rows * rows * blocks
    smem = pl.BlockSpec(memory_space=pltpu.SMEM)
    return pl.pallas_call(
        kernel,
        out_shape=out_shape,
        in_specs=[smem] * scalars + [VMEM] * (len(arrays) - scalars),
        out_specs=(VMEM,) * len(out_shape),
        compiler_params=pltpu.CompilerParams(vmem_limit_bytes=24 << 20),
        cost_estimate=pl.CostEstimate(
            flops=2 * products * HEAD_SIZE * pairs,
            bytes_accessed=2 * QUERY_HEADS * HEAD_SIZE * rows * products,
            transcendentals=(products - 1) * pairs,
        ),
        name=name,
    )(*arrays)


def own_maxima(rank, segments, queries, keys, reach):
    rows = queries.shape[0]
    out_shape = (
        jax.ShapeDtypeStruct((QUERY_HEADS, rows), jnp.float32),
        jax.ShapeDtypeStruct(((reach + 1) * rows, rows), jnp.float32),
    )
    kernel = functools.partial(own_max_kernel, reach)
    return call(
        kernel, "own_maxima", out_shape, 1, rows, 1, rank, segments, queries, keys, scalars=1
    )


def next_maxima(distance, bias, queries, row_max, keys, devices):
    rows = queries.shape[0]
    out_shape = (jax.ShapeDtypeStruct((QUERY_HEADS, rows), jnp.float32),)
    if devices:
        out_shape += (jax.ShapeDtypeStruct((devices, 1, rows), jnp.float32),)
    kernel = functools.partial(next_max_kernel, distance)
    name = f"maxima_{distance}"
    return call(kernel, name, out_shape, 1, rows, 1, bias, queries, row_max, keys)


def mix(bias, queries, row_max, key_blocks, value_blocks):
    reach, rows = len(key_blocks) - 1, queries.shape[0]
    out_shape = (jax.ShapeDtypeStruct(queries.shape, jnp.bfloat16),)
    kernel = functools.partial(mix_kernel, reach)
    arrays = (bias, queries, row_max, *key_blocks, *value_blocks)
    return call(kernel, "mix", out_shape, reach + 1, rows, 2, *arrays)[0]


def passed_along(x, by):
    shards = lax.axis_size("seq")
    return lax.ppermute(x, "seq", [(i, (i + by) % shards) for i in range(shards)])


def clip_factors(head_max):
    clipped_logits = clip_level / jnp.maximum(head_max, clip_level)
    key_head_factor = jnp.sqrt(jnp.min(clipped_logits.reshape(KEY_VALUE_HEADS, GROUP), axis=1))
    query_factor = clipped_logits / jnp.repeat(key_head_factor, GROUP)
    return (query_factor, key_head_factor)


def local(queries, keys, values, segments):
    rows, length = queries.shape[1], segments.shape[1]
    shards = lax.axis_size("seq")
    devices = lax.axis_size("dp") * shards
    reach = reach_of(rows, length, shards)
    rank = lax.axis_index("seq").astype(jnp.int32).reshape(1)
    queries, keys, values = queries[0], keys[0], values[0]

    distances = range(reach, 0, -1)
    key_blocks = {d: passed_along(keys, d) for d in distances}
    row_max, bias = own_maxima(rank, segments, queries, keys, reach)
    value_blocks = {}
    for d in distances:
        if d == 1:
            sent_values, row_max = lax.optimization_barrier((values, row_max))
            value_blocks = {d: passed_along(sent_values, d) for d in distances}
        row_max, *head_max = next_maxima(
            d, bias, queries, row_max, key_blocks[d], devices if d == 1 else 0
        )
    everyone = lax.all_to_all(head_max[0], ("dp", "seq"), 0, 0)
    attended = mix(
        bias,
        queries,
        row_max,
        [keys] + [key_blocks[d] for d in range(1, reach + 1)],
        [values] + [value_blocks[d] for d in range(1, reach + 1)],
    )
    query_factor, key_head_factor = clip_factors(
        jnp.max(everyone[:, 0, :QUERY_HEADS], axis=0)
    )
    return (attended[None], query_factor, key_head_factor)


def solution(mesh):
    in_specs = (P("dp", "seq", None), P("dp", "seq", None), P("dp", "seq", None), P("dp", None))
    out_specs = (P("dp", "seq", None), P(), P())
    return jax.shard_map(local, mesh=mesh, in_specs=in_specs, out_specs=out_specs, check_vma=False)
```

```python
import functools
import math

import jax
import jax.numpy as jnp
from jax import lax
from jax.experimental import pallas as pl
from jax.experimental.pallas import tpu as pltpu
from jax.sharding import PartitionSpec as P

QUERY_HEADS = 48
KEY_VALUE_HEADS = 6
HEAD_SIZE = 128
DOCUMENT_LIMIT = 384
GROUP = QUERY_HEADS // KEY_VALUE_HEADS

clip_level = 6.0
SCALE = HEAD_SIZE ** (-0.5)
SCALE_2 = SCALE * math.log2(math.e)
MASKED = -1e30
NT = (((1,), (1,)), ((), ()))


def reach_of(rows, length, shards):
    reach = (DOCUMENT_LIMIT - 1 + rows - 1) // rows
    documents = length // 256
    least = length - (documents - 1) * DOCUMENT_LIMIT
    if shards == reach + 1 and documents > 1 and least >= rows:
        reach -= 1
    return reach


def fill_bias(seg_ref, bias_ref, rank, shards, pairs, rows):
    docs = {}
    for behind in sorted({b for pair in pairs for b in pair[:2]}):
        block = jnp.clip(rank - behind, 0, shards - 1)
        at = pl.ds(pl.multiple_of(block * rows, rows), rows)
        docs[behind] = jnp.broadcast_to(seg_ref[:, at], (rows, rows))
    key_index = lax.broadcasted_iota(jnp.int32, (rows, rows), 0)
    query_index = lax.broadcasted_iota(jnp.int32, (rows, rows), 1)
    for place, (query_behind, key_behind, parity) in enumerate(pairs):
        valid = docs[key_behind].T == docs[query_behind]
        if key_behind == query_behind:
            valid = valid & (key_index <= query_index)
        valid = valid & (rank >= key_behind)
        if parity is not None:
            valid = valid & (rank % 2 == parity)
        bias_ref[place * rows : (place + 1) * rows, :] = jnp.where(valid, 0.0, MASKED)


def raise_maxima(max_ref, q_ref, key_ref, bias_ref, place, floor_ref=None):
    rows = q_ref.shape[0]
    bias = bias_ref[place * rows : (place + 1) * rows, :]
    for head in range(0, QUERY_HEADS, 2):
        column = head // GROUP
        keys = key_ref[:, column * HEAD_SIZE : (column + 1) * HEAD_SIZE]
        q = [q_ref[:, h * HEAD_SIZE : (h + 1) * HEAD_SIZE] for h in (head, head + 1)]
        logits = lax.dot_general(
            keys, jnp.concatenate(q, axis=0), NT, preferred_element_type=jnp.float32
        )
        for i in range(2):
            at = slice(head + i, head + i + 1)
            largest = jnp.max(logits[:, i * rows : (i + 1) * rows] + bias, axis=0, keepdims=True)
            if floor_ref is not None:
                largest = jnp.maximum(floor_ref[at, :], largest)
            max_ref[at, :] = largest


def store_head_maxima(head_max_ref, max_ref):
    largest = max_ref[...]
    rows = largest.shape[1]
    padded = jnp.concatenate([largest, largest, largest], axis=0)[:rows]
    head_max = jnp.max(padded.T, axis=0, keepdims=True) * SCALE
    head_max_ref[...] = jnp.broadcast_to(head_max[None], head_max_ref.shape)


def first_kernel(
    shards, pairs, seg_hbm, q_hbm, key_hbm, max_ref, bias_ref, q_ref, key_ref, seg_ref, sems
):
    copies = [
        pltpu.make_async_copy(source, target, sems.at[i])
        for i, (source, target) in enumerate(
            ((seg_hbm, seg_ref), (key_hbm, key_ref), (q_hbm, q_ref))
        )
    ]
    for copy in copies:
        copy.start()
    copies[0].wait()
    fill_bias(seg_ref, bias_ref, lax.axis_index("seq"), shards, pairs, q_ref.shape[0])
    copies[1].wait()
    copies[2].wait()
    raise_maxima(max_ref, q_ref, key_ref, bias_ref, 0)


def next_kernel(place, bias_ref, q_ref, before_ref, key_ref, max_ref, *head_max_refs):
    raise_maxima(max_ref, q_ref, key_ref, bias_ref, place, before_ref)
    for head_max_ref in head_max_refs:
        store_head_maxima(head_max_ref, max_ref)


def last_paired_kernel(
    bias_ref, q_ref, partner_ref, before_ref, near_ref, key_ref, max_ref, head_max_ref, all_ref
):
    raise_maxima(max_ref, q_ref, key_ref, bias_ref, 2, before_ref)
    raise_maxima(all_ref, partner_ref, key_ref, bias_ref, 3, near_ref)
    all_ref[...] = jnp.maximum(all_ref[...], max_ref[...])
    store_head_maxima(head_max_ref, all_ref)


def mix_kernel(blocks, bias_ref, q_ref, row_max_ref, *refs):
    key_refs, value_refs, out_ref = refs[:blocks], refs[blocks:-1], refs[-1]
    for column in range(KEY_VALUE_HEADS):
        at = slice(column * HEAD_SIZE, (column + 1) * HEAD_SIZE)
        key_block = jnp.concatenate([k[:, at] for k in key_refs], axis=0)
        value_block = jnp.concatenate([v[:, at].T for v in value_refs], axis=1)
        for head in range(column * GROUP, (column + 1) * GROUP):
            here = slice(head * HEAD_SIZE, (head + 1) * HEAD_SIZE)
            logits = lax.dot_general(
                key_block, q_ref[:, here], NT, preferred_element_type=jnp.float32
            )
            largest = row_max_ref[head : head + 1, :] * SCALE_2
            expo = jnp.exp2((logits + bias_ref[: key_block.shape[0], :]) * SCALE_2 - largest)
            share = 1.0 / jnp.sum(expo, axis=0, keepdims=True)
            mixed = jnp.dot(
                value_block, expo.astype(jnp.bfloat16), preferred_element_type=jnp.float32
            )
            out_ref[:, here] = (mixed * share).astype(jnp.bfloat16).T


def mix_paired_kernel(bias_ref, q_ref, row_max_ref, own, near, far, *refs):
    *value_refs, out_ref, max_ref = refs
    raise_maxima(max_ref, q_ref, near, bias_ref, 1, row_max_ref)
    mix_kernel(3, bias_ref, q_ref, max_ref, own, near, far, *value_refs, out_ref)


VMEM = pl.BlockSpec(memory_space=pltpu.VMEM)


def call(kernel, name, out_shape, blocks, products, *arrays, scratch=()):
    rows = out_shape[0].shape[-1] if products == 1 else out_shape[0].shape[0]
    pairs = QUERY_HEADS * rows * rows * blocks
    return pl.pallas_call(
        kernel,
        out_shape=out_shape,
        in_specs=[VMEM] * len(arrays),
        out_specs=(VMEM,) * len(out_shape),
        scratch_shapes=scratch,
        compiler_params=pltpu.CompilerParams(vmem_limit_bytes=24 << 20),
        cost_estimate=pl.CostEstimate(
            flops=2 * products * HEAD_SIZE * pairs,
            bytes_accessed=2 * QUERY_HEADS * HEAD_SIZE * rows * products,
            transcendentals=(products - 1) * pairs,
        ),
        name=name,
    )(*arrays)


def first_maxima(shards, pairs, segments, queries, keys):
    rows = queries.shape[0]
    hbm = pl.BlockSpec(memory_space=pltpu.HBM)
    out_shape = (
        pltpu.VMEM((QUERY_HEADS, rows), jnp.float32),
        pltpu.VMEM((len(pairs) * rows, rows), jnp.float32),
        pltpu.VMEM(queries.shape, queries.dtype),
        pltpu.VMEM(keys.shape, keys.dtype),
    )
    operands = [
        pltpu.with_memory_space_constraint(x, pltpu.HBM) for x in (segments, queries, keys)
    ]
    return pl.pallas_call(
        functools.partial(first_kernel, shards, pairs),
        out_shape=out_shape,
        in_specs=[hbm] * 3,
        out_specs=(VMEM,) * 4,
        scratch_shapes=[
            pltpu.VMEM(segments.shape, segments.dtype),
            pltpu.SemaphoreType.DMA((3,)),
        ],
        compiler_params=pltpu.CompilerParams(vmem_limit_bytes=24 << 20),
        cost_estimate=pl.CostEstimate(
            flops=2 * QUERY_HEADS * HEAD_SIZE * rows * rows,
            bytes_accessed=2 * QUERY_HEADS * HEAD_SIZE * rows,
            transcendentals=0,
        ),
        name="first_maxima",
    )(*operands)


def in_vmem(x):
    return pltpu.with_memory_space_constraint(x, pltpu.VMEM)


def float32(*shape):
    return jax.ShapeDtypeStruct(shape, jnp.float32)


def like(x):
    return jax.ShapeDtypeStruct(x.shape, x.dtype)


def plan_of_pairs(segments, queries, keys, values, devices):
    rows = queries.shape[0]
    across = [(i, i ^ 2) for i in range(4)]
    swap = [(i, i ^ 1) for i in range(4)]
    rotate = [(i, (i + 1) % 4) for i in range(4)]
    far_keys = lax.ppermute(keys, "seq", across)
    partner_queries = lax.ppermute(queries, "seq", swap)
    pairs = ((0, 0, None), (0, 1, None), (0, 2, None), (1, 2, 1), (-1, 0, 0))
    max_shape = float32(QUERY_HEADS, rows)
    row_max, bias, queries, own_keys = first_maxima(4, pairs, segments, queries, keys)
    sent_keys, values, bias = lax.optimization_barrier((keys, values, bias))
    far_values = lax.ppermute(values, "seq", across)
    near_values = lax.ppermute(values, "seq", rotate)
    near_keys = lax.ppermute(sent_keys, "seq", rotate)
    (near_max,) = call(
        functools.partial(next_kernel, 4),
        "near_maxima",
        (max_shape,),
        1,
        1,
        bias,
        partner_queries,
        row_max,
        own_keys,
    )
    row_max, head_max = call(
        last_paired_kernel,
        "last_maxima",
        (max_shape, float32(devices, 1, rows)),
        2,
        1,
        bias,
        queries,
        partner_queries,
        row_max,
        near_max,
        in_vmem(far_keys),
        scratch=[pltpu.VMEM(max_shape.shape, jnp.float32)],
    )
    everyone = lax.all_to_all(head_max, ("dp", "seq"), 0, 0)
    (attended,) = call(
        mix_paired_kernel,
        "mix",
        (like(queries),),
        3,
        2,
        bias,
        queries,
        row_max,
        own_keys,
        in_vmem(near_keys),
        in_vmem(far_keys),
        in_vmem(values),
        in_vmem(near_values),
        in_vmem(far_values),
        scratch=[pltpu.VMEM(max_shape.shape, jnp.float32)],
    )
    return attended, everyone


def plan_of_rotations(segments, queries, keys, values, devices, reach, shards):
    def passed_along(x, by):
        return lax.ppermute(x, "seq", [(i, (i + by) % shards) for i in range(shards)])

    rows = queries.shape[0]
    distances = range(reach, 0, -1)
    key_blocks = {d: passed_along(keys, d) for d in distances}
    pairs = tuple((0, d, None) for d in range(reach + 1))
    max_shape = float32(QUERY_HEADS, rows)
    row_max, bias, queries, own_keys = first_maxima(
        shards, pairs, segments, queries, keys
    )
    sent_values, bias = lax.optimization_barrier((values, bias))
    value_blocks = {d: passed_along(sent_values, d) for d in distances}
    for d in distances:
        out_shape = (max_shape,) + ((float32(devices, 1, rows),) if d == 1 else ())
        row_max, *head_max = call(
            functools.partial(next_kernel, d),
            f"maxima_{d}",
            out_shape,
            1,
            1,
            bias,
            queries,
            row_max,
            key_blocks[d],
        )
    everyone = lax.all_to_all(head_max[0], ("dp", "seq"), 0, 0)
    (attended,) = call(
        functools.partial(mix_kernel, reach + 1),
        "mix",
        (like(queries),),
        reach + 1,
        2,
        bias,
        queries,
        row_max,
        own_keys,
        *[key_blocks[d] for d in range(1, reach + 1)],
        values,
        *[value_blocks[d] for d in range(1, reach + 1)],
    )
    return attended, everyone


def clip_factors(head_max):
    clipped_logits = clip_level / jnp.maximum(head_max, clip_level)
    key_head_factor = jnp.sqrt(jnp.min(clipped_logits.reshape(KEY_VALUE_HEADS, GROUP), axis=1))
    query_factor = clipped_logits / jnp.repeat(key_head_factor, GROUP)
    return (query_factor, key_head_factor)


def local(queries, keys, values, segments):
    rows, length = queries.shape[1], segments.shape[1]
    shards = lax.axis_size("seq")
    devices = lax.axis_size("dp") * shards
    reach = reach_of(rows, length, shards)
    arrays = (segments, queries[0], keys[0], values[0], devices)
    if shards == 4 and reach == 2:
        attended, everyone = plan_of_pairs(*arrays)
    else:
        attended, everyone = plan_of_rotations(*arrays, reach, shards)
    everyone, attended = lax.optimization_barrier((everyone, attended))
    query_factor, key_head_factor = clip_factors(
        jnp.max(everyone[:, 0, :QUERY_HEADS], axis=0)
    )
    return (attended[None], query_factor, key_head_factor)


def solution(mesh):
    in_specs = (P("dp", "seq", None), P("dp", "seq", None), P("dp", "seq", None), P("dp", None))
    out_specs = (P("dp", "seq", None), P(), P())
    return jax.shard_map(local, mesh=mesh, in_specs=in_specs, out_specs=out_specs, check_vma=False)
```

```python
import functools
import math

import jax
import jax.numpy as jnp
from jax import lax
from jax.experimental import pallas as pl
from jax.experimental.pallas import tpu as pltpu
from jax.sharding import PartitionSpec as P

QUERY_HEADS = 48
KEY_VALUE_HEADS = 6
HEAD_SIZE = 128
DOCUMENT_LIMIT = 384
GROUP = QUERY_HEADS // KEY_VALUE_HEADS

clip_level = 6.0
SCALE = HEAD_SIZE ** (-0.5)
SCALE_2 = SCALE * math.log2(math.e)
MASKED = -1e30
NT = (((1,), (1,)), ((), ()))


def reach_of(rows, length, shards):
    reach = (DOCUMENT_LIMIT - 1 + rows - 1) // rows
    documents = length // 256
    least = length - (documents - 1) * DOCUMENT_LIMIT
    if shards == reach + 1 and documents > 1 and least >= rows:
        reach -= 1
    return reach


def fill_bias(seg_ref, bias_ref, rank, shards, pairs, rows):
    docs = {}
    for behind in sorted({b for pair in pairs for b in pair[:2]}):
        block = jnp.clip(rank - behind, 0, shards - 1)
        at = pl.ds(pl.multiple_of(block * rows, rows), rows)
        docs[behind] = jnp.broadcast_to(seg_ref[:, at], (rows, rows))
    key_index = lax.broadcasted_iota(jnp.int32, (rows, rows), 0)
    query_index = lax.broadcasted_iota(jnp.int32, (rows, rows), 1)
    for place, (query_behind, key_behind, parity) in enumerate(pairs):
        valid = docs[key_behind].T == docs[query_behind]
        if key_behind == query_behind:
            valid = valid & (key_index <= query_index)
        valid = valid & (rank >= key_behind)
        if parity is not None:
            valid = valid & (rank % 2 == parity)
        bias_ref[place * rows : (place + 1) * rows, :] = jnp.where(valid, 0.0, MASKED)


def raise_maxima(max_ref, q_ref, key_ref, bias_ref, place, floor_ref=None):
    rows = q_ref.shape[0]
    bias = bias_ref[place * rows : (place + 1) * rows, :]
    for head in range(0, QUERY_HEADS, 2):
        column = head // GROUP
        keys = key_ref[:, column * HEAD_SIZE : (column + 1) * HEAD_SIZE]
        q = [q_ref[:, h * HEAD_SIZE : (h + 1) * HEAD_SIZE] for h in (head, head + 1)]
        logits = lax.dot_general(
            keys, jnp.concatenate(q, axis=0), NT, preferred_element_type=jnp.float32
        )
        for i in range(2):
            at = slice(head + i, head + i + 1)
            largest = jnp.max(logits[:, i * rows : (i + 1) * rows] + bias, axis=0, keepdims=True)
            if floor_ref is not None:
                largest = jnp.maximum(floor_ref[at, :], largest)
            max_ref[at, :] = largest


def store_head_maxima(head_max_ref, max_ref):
    largest = max_ref[...]
    rows = largest.shape[1]
    padded = jnp.concatenate([largest, largest, largest], axis=0)[:rows]
    head_max = jnp.max(padded.T, axis=0, keepdims=True) * SCALE
    head_max_ref[...] = jnp.broadcast_to(head_max[None], head_max_ref.shape)


def first_kernel(
    shards, pairs, seg_hbm, q_hbm, key_hbm, max_ref, bias_ref, q_ref, key_ref, seg_ref, sems
):
    copies = [
        pltpu.make_async_copy(source, target, sems.at[i])
        for i, (source, target) in enumerate(
            ((seg_hbm, seg_ref), (key_hbm, key_ref), (q_hbm, q_ref))
        )
    ]
    for copy in copies:
        copy.start()
    copies[0].wait()
    fill_bias(seg_ref, bias_ref, lax.axis_index("seq"), shards, pairs, q_ref.shape[0])
    copies[1].wait()
    copies[2].wait()
    raise_maxima(max_ref, q_ref, key_ref, bias_ref, 0)


def next_kernel(place, bias_ref, q_ref, before_ref, key_ref, max_ref, *head_max_refs):
    raise_maxima(max_ref, q_ref, key_ref, bias_ref, place, before_ref)
    for head_max_ref in head_max_refs:
        store_head_maxima(head_max_ref, max_ref)


def last_paired_kernel(
    bias_ref, q_ref, partner_ref, before_ref, near_ref, key_ref, max_ref, head_max_ref, all_ref
):
    raise_maxima(max_ref, q_ref, key_ref, bias_ref, 2, before_ref)
    all_ref[...] = jnp.maximum(near_ref[...], max_ref[...])

    @pl.when(lax.axis_index("seq") % 2 == 1)
    def _():
        raise_maxima(all_ref, partner_ref, key_ref, bias_ref, 3, all_ref)

    store_head_maxima(head_max_ref, all_ref)


def mix_kernel(blocks, bias_ref, q_ref, row_max_ref, *refs):
    key_refs, value_refs, out_ref = refs[:blocks], refs[blocks:-1], refs[-1]
    for column in range(KEY_VALUE_HEADS):
        at = slice(column * HEAD_SIZE, (column + 1) * HEAD_SIZE)
        key_block = jnp.concatenate([k[:, at] for k in key_refs], axis=0)
        value_block = jnp.concatenate([v[:, at].T for v in value_refs], axis=1)
        for head in range(column * GROUP, (column + 1) * GROUP):
            here = slice(head * HEAD_SIZE, (head + 1) * HEAD_SIZE)
            logits = lax.dot_general(
                key_block, q_ref[:, here], NT, preferred_element_type=jnp.float32
            )
            largest = row_max_ref[head : head + 1, :] * SCALE_2
            expo = jnp.exp2((logits + bias_ref[: key_block.shape[0], :]) * SCALE_2 - largest)
            share = 1.0 / jnp.sum(expo, axis=0, keepdims=True)
            mixed = jnp.dot(
                value_block, expo.astype(jnp.bfloat16), preferred_element_type=jnp.float32
            )
            out_ref[:, here] = (mixed * share).astype(jnp.bfloat16).T


def mix_paired_kernel(bias_ref, q_ref, row_max_ref, own, near, far, *refs):
    *value_refs, out_ref, max_ref = refs
    raise_maxima(max_ref, q_ref, near, bias_ref, 1, row_max_ref)
    mix_kernel(3, bias_ref, q_ref, max_ref, own, near, far, *value_refs, out_ref)


VMEM = pl.BlockSpec(memory_space=pltpu.VMEM)


def call(kernel, name, out_shape, blocks, products, *arrays, scratch=()):
    rows = out_shape[0].shape[-1] if products == 1 else out_shape[0].shape[0]
    pairs = QUERY_HEADS * rows * rows * blocks
    return pl.pallas_call(
        kernel,
        out_shape=out_shape,
        in_specs=[VMEM] * len(arrays),
        out_specs=(VMEM,) * len(out_shape),
        scratch_shapes=scratch,
        compiler_params=pltpu.CompilerParams(vmem_limit_bytes=24 << 20),
        cost_estimate=pl.CostEstimate(
            flops=2 * products * HEAD_SIZE * pairs,
            bytes_accessed=2 * QUERY_HEADS * HEAD_SIZE * rows * products,
            transcendentals=(products - 1) * pairs,
        ),
        name=name,
    )(*arrays)


def first_maxima(shards, pairs, segments, queries, keys):
    rows = queries.shape[0]
    hbm = pl.BlockSpec(memory_space=pltpu.HBM)
    out_shape = (
        pltpu.VMEM((QUERY_HEADS, rows), jnp.float32),
        pltpu.VMEM((len(pairs) * rows, rows), jnp.float32),
        pltpu.VMEM(queries.shape, queries.dtype),
        pltpu.VMEM(keys.shape, keys.dtype),
    )
    operands = [
        pltpu.with_memory_space_constraint(x, pltpu.HBM) for x in (segments, queries, keys)
    ]
    return pl.pallas_call(
        functools.partial(first_kernel, shards, pairs),
        out_shape=out_shape,
        in_specs=[hbm] * 3,
        out_specs=(VMEM,) * 4,
        scratch_shapes=[
            pltpu.VMEM(segments.shape, segments.dtype),
            pltpu.SemaphoreType.DMA((3,)),
        ],
        compiler_params=pltpu.CompilerParams(vmem_limit_bytes=24 << 20),
        cost_estimate=pl.CostEstimate(
            flops=2 * QUERY_HEADS * HEAD_SIZE * rows * rows,
            bytes_accessed=2 * QUERY_HEADS * HEAD_SIZE * rows,
            transcendentals=0,
        ),
        name="first_maxima",
    )(*operands)


def in_vmem(x):
    return pltpu.with_memory_space_constraint(x, pltpu.VMEM)


def float32(*shape):
    return jax.ShapeDtypeStruct(shape, jnp.float32)


def like(x):
    return jax.ShapeDtypeStruct(x.shape, x.dtype)


def plan_of_pairs(segments, queries, keys, values, devices):
    rows = queries.shape[0]
    across = [(i, i ^ 2) for i in range(4)]
    swap = [(i, i ^ 1) for i in range(4)]
    rotate = [(i, (i + 1) % 4) for i in range(4)]
    far_keys = lax.ppermute(keys, "seq", across)
    partner_queries = lax.ppermute(queries, "seq", swap)
    pairs = ((0, 0, None), (0, 1, None), (0, 2, None), (1, 2, 1), (-1, 0, 0))
    max_shape = float32(QUERY_HEADS, rows)
    row_max, bias, queries, own_keys = first_maxima(4, pairs, segments, queries, keys)
    (near_max,) = call(
        functools.partial(next_kernel, 4),
        "near_maxima",
        (max_shape,),
        1,
        1,
        bias,
        partner_queries,
        row_max,
        own_keys,
    )
    sent_keys, values, near_max = lax.optimization_barrier((keys, values, near_max))
    far_values = lax.ppermute(values, "seq", across)
    near_values = lax.ppermute(values, "seq", rotate)
    near_keys = lax.ppermute(sent_keys, "seq", rotate)
    row_max, head_max = call(
        last_paired_kernel,
        "last_maxima",
        (max_shape, pltpu.VMEM((devices, 1, rows), jnp.float32)),
        2,
        1,
        bias,
        queries,
        partner_queries,
        row_max,
        near_max,
        in_vmem(far_keys),
        scratch=[pltpu.VMEM(max_shape.shape, jnp.float32)],
    )
    everyone = lax.all_to_all(head_max, ("dp", "seq"), 0, 0)
    (attended,) = call(
        mix_paired_kernel,
        "mix",
        (like(queries),),
        3,
        2,
        bias,
        queries,
        row_max,
        own_keys,
        in_vmem(near_keys),
        in_vmem(far_keys),
        in_vmem(values),
        in_vmem(near_values),
        in_vmem(far_values),
        scratch=[pltpu.VMEM(max_shape.shape, jnp.float32)],
    )
    return attended, everyone


def plan_of_rotations(segments, queries, keys, values, devices, reach, shards):
    def passed_along(x, by):
        return lax.ppermute(x, "seq", [(i, (i + by) % shards) for i in range(shards)])

    rows = queries.shape[0]
    distances = range(reach, 0, -1)
    key_blocks = {d: passed_along(keys, d) for d in distances}
    pairs = tuple((0, d, None) for d in range(reach + 1))
    max_shape = float32(QUERY_HEADS, rows)
    row_max, bias, queries, own_keys = first_maxima(
        shards, pairs, segments, queries, keys
    )
    sent_values, bias = lax.optimization_barrier((values, bias))
    value_blocks = {d: passed_along(sent_values, d) for d in distances}
    for d in distances:
        out_shape = (max_shape,) + ((float32(devices, 1, rows),) if d == 1 else ())
        row_max, *head_max = call(
            functools.partial(next_kernel, d),
            f"maxima_{d}",
            out_shape,
            1,
            1,
            bias,
            queries,
            row_max,
            key_blocks[d],
        )
    everyone = lax.all_to_all(head_max[0], ("dp", "seq"), 0, 0)
    (attended,) = call(
        functools.partial(mix_kernel, reach + 1),
        "mix",
        (like(queries),),
        reach + 1,
        2,
        bias,
        queries,
        row_max,
        own_keys,
        *[key_blocks[d] for d in range(1, reach + 1)],
        values,
        *[value_blocks[d] for d in range(1, reach + 1)],
    )
    return attended, everyone


def clip_factors(head_max):
    clipped_logits = clip_level / jnp.maximum(head_max, clip_level)
    key_head_factor = jnp.sqrt(jnp.min(clipped_logits.reshape(KEY_VALUE_HEADS, GROUP), axis=1))
    query_factor = clipped_logits / jnp.repeat(key_head_factor, GROUP)
    return (query_factor, key_head_factor)


def local(queries, keys, values, segments):
    rows, length = queries.shape[1], segments.shape[1]
    shards = lax.axis_size("seq")
    devices = lax.axis_size("dp") * shards
    reach = reach_of(rows, length, shards)
    arrays = (segments, queries[0], keys[0], values[0], devices)
    if shards == 4 and reach == 2:
        attended, everyone = plan_of_pairs(*arrays)
    else:
        attended, everyone = plan_of_rotations(*arrays, reach, shards)
    everyone, attended = lax.optimization_barrier((everyone, attended))
    query_factor, key_head_factor = clip_factors(
        jnp.max(everyone[:, 0, :QUERY_HEADS], axis=0)
    )
    return (attended[None], query_factor, key_head_factor)


def solution(mesh):
    in_specs = (P("dp", "seq", None), P("dp", "seq", None), P("dp", "seq", None), P("dp", None))
    out_specs = (P("dp", "seq", None), P(), P())
    return jax.shard_map(local, mesh=mesh, in_specs=in_specs, out_specs=out_specs, check_vma=False)
```

```python
import functools
import math

import jax
import jax.numpy as jnp
from jax import lax
from jax.experimental import pallas as pl
from jax.experimental.pallas import tpu as pltpu
from jax.sharding import PartitionSpec as P

QUERY_HEADS = 48
KEY_VALUE_HEADS = 6
HEAD_SIZE = 128
DOCUMENT_LIMIT = 384
GROUP = QUERY_HEADS // KEY_VALUE_HEADS

clip_level = 6.0
SCALE = HEAD_SIZE ** (-0.5)
SCALE_2 = SCALE * math.log2(math.e)
MASKED = -1e30
NT = (((1,), (1,)), ((), ()))


def reach_of(rows, length, shards):
    reach = (DOCUMENT_LIMIT - 1 + rows - 1) // rows
    documents = length // 256
    least = length - (documents - 1) * DOCUMENT_LIMIT
    if shards == reach + 1 and documents > 1 and least >= rows:
        reach -= 1
    return reach


def fill_bias(seg_ref, bias_ref, rank, shards, pairs, rows):
    docs = {}
    for behind in sorted({b for pair in pairs for b in pair[:2]}):
        block = jnp.clip(rank - behind, 0, shards - 1)
        at = pl.ds(pl.multiple_of(block * rows, rows), rows)
        docs[behind] = jnp.broadcast_to(seg_ref[:, at], (rows, rows))
    key_index = lax.broadcasted_iota(jnp.int32, (rows, rows), 0)
    query_index = lax.broadcasted_iota(jnp.int32, (rows, rows), 1)
    for place, (query_behind, key_behind, parity) in enumerate(pairs):
        valid = docs[key_behind].T == docs[query_behind]
        if key_behind == query_behind:
            valid = valid & (key_index <= query_index)
        valid = valid & (rank >= key_behind)
        if parity is not None:
            valid = valid & (rank % 2 == parity)
        bias_ref[place * rows : (place + 1) * rows, :] = jnp.where(valid, 0.0, MASKED)


def raise_maxima(max_ref, q_ref, key_ref, bias_ref, place, floor_ref=None):
    rows = q_ref.shape[0]
    bias = bias_ref[place * rows : (place + 1) * rows, :]
    for head in range(0, QUERY_HEADS, 2):
        column = head // GROUP
        keys = key_ref[:, column * HEAD_SIZE : (column + 1) * HEAD_SIZE]
        q = [q_ref[:, h * HEAD_SIZE : (h + 1) * HEAD_SIZE] for h in (head, head + 1)]
        logits = lax.dot_general(
            keys, jnp.concatenate(q, axis=0), NT, preferred_element_type=jnp.float32
        )
        for i in range(2):
            at = slice(head + i, head + i + 1)
            largest = jnp.max(logits[:, i * rows : (i + 1) * rows] + bias, axis=0, keepdims=True)
            if floor_ref is not None:
                largest = jnp.maximum(floor_ref[at, :], largest)
            max_ref[at, :] = largest


def store_head_maxima(head_max_ref, max_ref):
    largest = max_ref[...]
    rows = largest.shape[1]
    padded = jnp.concatenate([largest, largest, largest], axis=0)[:rows]
    head_max = jnp.max(padded.T, axis=0, keepdims=True) * SCALE
    head_max_ref[...] = jnp.broadcast_to(head_max[None], head_max_ref.shape)


def load_kernel(
    shards, pairs, seg_hbm, q_hbm, key_hbm, bias_ref, q_ref, key_ref, seg_ref, sems
):
    copies = [
        pltpu.make_async_copy(source, target, sems.at[i])
        for i, (source, target) in enumerate(
            ((seg_hbm, seg_ref), (key_hbm, key_ref), (q_hbm, q_ref))
        )
    ]
    for copy in copies:
        copy.start()
    copies[0].wait()
    fill_bias(seg_ref, bias_ref, lax.axis_index("seq"), shards, pairs, q_ref.shape[0])
    copies[1].wait()
    copies[2].wait()


def first_kernel(bias_ref, q_ref, key_ref, *refs):
    *partner_ref, max_ref = refs[: len(refs) // 2 + 1]
    raise_maxima(max_ref, q_ref, key_ref, bias_ref, 0)
    if partner_ref:
        raise_maxima(refs[-1], partner_ref[0], key_ref, bias_ref, 4, max_ref)


def next_kernel(place, bias_ref, q_ref, before_ref, key_ref, max_ref, *head_max_refs):
    raise_maxima(max_ref, q_ref, key_ref, bias_ref, place, before_ref)
    for head_max_ref in head_max_refs:
        store_head_maxima(head_max_ref, max_ref)


def last_paired_kernel(
    bias_ref, q_ref, partner_ref, before_ref, near_ref, key_ref, max_ref, head_max_ref, all_ref
):
    raise_maxima(max_ref, q_ref, key_ref, bias_ref, 2, before_ref)
    all_ref[...] = jnp.maximum(near_ref[...], max_ref[...])

    @pl.when(lax.axis_index("seq") % 2 == 1)
    def _():
        raise_maxima(all_ref, partner_ref, key_ref, bias_ref, 3, all_ref)

    store_head_maxima(head_max_ref, all_ref)


def mix_kernel(blocks, bias_ref, q_ref, row_max_ref, *refs):
    key_refs, value_refs, out_ref = refs[:blocks], refs[blocks:-1], refs[-1]
    for column in range(KEY_VALUE_HEADS):
        at = slice(column * HEAD_SIZE, (column + 1) * HEAD_SIZE)
        key_block = jnp.concatenate([k[:, at] for k in key_refs], axis=0)
        value_block = jnp.concatenate([v[:, at].T for v in value_refs], axis=1)
        for head in range(column * GROUP, (column + 1) * GROUP):
            here = slice(head * HEAD_SIZE, (head + 1) * HEAD_SIZE)
            logits = lax.dot_general(
                key_block, q_ref[:, here], NT, preferred_element_type=jnp.float32
            )
            largest = row_max_ref[head : head + 1, :] * SCALE_2
            expo = jnp.exp2((logits + bias_ref[: key_block.shape[0], :]) * SCALE_2 - largest)
            share = 1.0 / jnp.sum(expo, axis=0, keepdims=True)
            mixed = jnp.dot(
                value_block, expo.astype(jnp.bfloat16), preferred_element_type=jnp.float32
            )
            out_ref[:, here] = (mixed * share).astype(jnp.bfloat16).T


def mix_paired_kernel(bias_ref, q_ref, row_max_ref, own, near, far, *refs):
    *value_refs, out_ref, max_ref = refs
    raise_maxima(max_ref, q_ref, near, bias_ref, 1, row_max_ref)
    mix_kernel(3, bias_ref, q_ref, max_ref, own, near, far, *value_refs, out_ref)


VMEM = pl.BlockSpec(memory_space=pltpu.VMEM)


def call(kernel, name, out_shape, blocks, products, *arrays, scratch=()):
    rows = out_shape[0].shape[-1] if products == 1 else out_shape[0].shape[0]
    pairs = QUERY_HEADS * rows * rows * blocks
    return pl.pallas_call(
        kernel,
        out_shape=out_shape,
        in_specs=[VMEM] * len(arrays),
        out_specs=(VMEM,) * len(out_shape),
        scratch_shapes=scratch,
        compiler_params=pltpu.CompilerParams(vmem_limit_bytes=24 << 20),
        cost_estimate=pl.CostEstimate(
            flops=2 * products * HEAD_SIZE * pairs,
            bytes_accessed=2 * QUERY_HEADS * HEAD_SIZE * rows * products,
            transcendentals=(products - 1) * pairs,
        ),
        name=name,
    )(*arrays)


def load(shards, pairs, segments, queries, keys):
    rows = queries.shape[0]
    hbm = pl.BlockSpec(memory_space=pltpu.HBM)
    operands = [
        pltpu.with_memory_space_constraint(x, pltpu.HBM) for x in (segments, queries, keys)
    ]
    return pl.pallas_call(
        functools.partial(load_kernel, shards, pairs),
        out_shape=(
            pltpu.VMEM((len(pairs) * rows, rows), jnp.float32),
            pltpu.VMEM(queries.shape, queries.dtype),
            pltpu.VMEM(keys.shape, keys.dtype),
        ),
        in_specs=[hbm] * 3,
        out_specs=(VMEM,) * 3,
        scratch_shapes=[
            pltpu.VMEM(segments.shape, segments.dtype),
            pltpu.SemaphoreType.DMA((3,)),
        ],
        compiler_params=pltpu.CompilerParams(vmem_limit_bytes=24 << 20),
        cost_estimate=pl.CostEstimate(
            flops=0, bytes_accessed=2 * (queries.size + keys.size), transcendentals=0
        ),
        name="load",
    )(*operands)


def in_vmem(x):
    return pltpu.with_memory_space_constraint(x, pltpu.VMEM)


def float32(*shape):
    return jax.ShapeDtypeStruct(shape, jnp.float32)


def like(x):
    return jax.ShapeDtypeStruct(x.shape, x.dtype)


def plan_of_pairs(segments, queries, keys, values, devices):
    rows = queries.shape[0]
    across = [(i, i ^ 2) for i in range(4)]
    swap = [(i, i ^ 1) for i in range(4)]
    rotate = [(i, (i + 1) % 4) for i in range(4)]
    far_keys = lax.ppermute(keys, "seq", across)
    partner_queries = lax.ppermute(queries, "seq", swap)
    pairs = ((0, 0, None), (0, 1, None), (0, 2, None), (1, 2, 1), (-1, 0, 0))
    max_shape = float32(QUERY_HEADS, rows)
    bias, queries, own_keys = load(4, pairs, segments, queries, keys)
    row_max, near_max = call(
        first_kernel,
        "first_maxima",
        (max_shape, max_shape),
        2,
        1,
        bias,
        queries,
        own_keys,
        partner_queries,
    )
    sent_keys, values, near_max = lax.optimization_barrier((keys, values, near_max))
    far_values = lax.ppermute(values, "seq", across)
    near_values = lax.ppermute(values, "seq", rotate)
    near_keys = lax.ppermute(sent_keys, "seq", rotate)
    row_max, head_max = call(
        last_paired_kernel,
        "last_maxima",
        (max_shape, pltpu.VMEM((devices, 1, rows), jnp.float32)),
        2,
        1,
        bias,
        queries,
        partner_queries,
        row_max,
        near_max,
        in_vmem(far_keys),
        scratch=[pltpu.VMEM(max_shape.shape, jnp.float32)],
    )
    everyone = lax.all_to_all(head_max, ("dp", "seq"), 0, 0)
    (attended,) = call(
        mix_paired_kernel,
        "mix",
        (like(queries),),
        3,
        2,
        bias,
        queries,
        row_max,
        own_keys,
        in_vmem(near_keys),
        in_vmem(far_keys),
        in_vmem(values),
        in_vmem(near_values),
        in_vmem(far_values),
        scratch=[pltpu.VMEM(max_shape.shape, jnp.float32)],
    )
    return attended, everyone


def plan_of_rotations(segments, queries, keys, values, devices, reach, shards):
    def passed_along(x, by):
        return lax.ppermute(x, "seq", [(i, (i + by) % shards) for i in range(shards)])

    rows = queries.shape[0]
    distances = range(reach, 0, -1)
    key_blocks = {d: passed_along(keys, d) for d in distances}
    pairs = tuple((0, d, None) for d in range(reach + 1))
    max_shape = float32(QUERY_HEADS, rows)
    bias, queries, own_keys = load(shards, pairs, segments, queries, keys)
    (row_max,) = call(
        first_kernel, "first_maxima", (max_shape,), 1, 1, bias, queries, own_keys
    )
    sent_values, bias = lax.optimization_barrier((values, bias))
    value_blocks = {d: passed_along(sent_values, d) for d in distances}
    for d in distances:
        out_shape = (max_shape,) + ((float32(devices, 1, rows),) if d == 1 else ())
        row_max, *head_max = call(
            functools.partial(next_kernel, d),
            f"maxima_{d}",
            out_shape,
            1,
            1,
            bias,
            queries,
            row_max,
            key_blocks[d],
        )
    everyone = lax.all_to_all(head_max[0], ("dp", "seq"), 0, 0)
    (attended,) = call(
        functools.partial(mix_kernel, reach + 1),
        "mix",
        (like(queries),),
        reach + 1,
        2,
        bias,
        queries,
        row_max,
        own_keys,
        *[key_blocks[d] for d in range(1, reach + 1)],
        values,
        *[value_blocks[d] for d in range(1, reach + 1)],
    )
    return attended, everyone


def clip_factors(head_max):
    clipped_logits = clip_level / jnp.maximum(head_max, clip_level)
    key_head_factor = jnp.sqrt(jnp.min(clipped_logits.reshape(KEY_VALUE_HEADS, GROUP), axis=1))
    query_factor = clipped_logits / jnp.repeat(key_head_factor, GROUP)
    return (query_factor, key_head_factor)


def local(queries, keys, values, segments):
    rows, length = queries.shape[1], segments.shape[1]
    shards = lax.axis_size("seq")
    devices = lax.axis_size("dp") * shards
    reach = reach_of(rows, length, shards)
    arrays = (segments, queries[0], keys[0], values[0], devices)
    if shards == 4 and reach == 2:
        attended, everyone = plan_of_pairs(*arrays)
    else:
        attended, everyone = plan_of_rotations(*arrays, reach, shards)
    everyone, attended = lax.optimization_barrier((everyone, attended))
    query_factor, key_head_factor = clip_factors(
        jnp.max(everyone[:, 0, :QUERY_HEADS], axis=0)
    )
    return (attended[None], query_factor, key_head_factor)


def solution(mesh):
    in_specs = (P("dp", "seq", None), P("dp", "seq", None), P("dp", "seq", None), P("dp", None))
    out_specs = (P("dp", "seq", None), P(), P())
    return jax.shard_map(local, mesh=mesh, in_specs=in_specs, out_specs=out_specs, check_vma=False)
```

```python
import functools
import math

import jax
import jax.numpy as jnp
from jax import lax
from jax.experimental import pallas as pl
from jax.experimental.pallas import tpu as pltpu
from jax.sharding import PartitionSpec as P

QUERY_HEADS = 48
KEY_VALUE_HEADS = 6
HEAD_SIZE = 128
DOCUMENT_LIMIT = 384
GROUP = QUERY_HEADS // KEY_VALUE_HEADS

clip_level = 6.0
SCALE = HEAD_SIZE ** (-0.5)
SCALE_2 = SCALE * math.log2(math.e)
MASKED = -1e30
KEY_HEAD_LANE = 64
NT = (((1,), (1,)), ((), ()))


def reach_of(rows, length, shards):
    reach = (DOCUMENT_LIMIT - 1 + rows - 1) // rows
    documents = length // 256
    least = length - (documents - 1) * DOCUMENT_LIMIT
    if shards == reach + 1 and documents > 1 and least >= rows:
        reach -= 1
    return reach


def fill_bias(seg_ref, bias_ref, rank, shards, pairs, rows):
    docs = {}
    for behind in sorted({b for pair in pairs for b in pair[:2]}):
        block = jnp.clip(rank - behind, 0, shards - 1)
        at = pl.ds(pl.multiple_of(block * rows, rows), rows)
        docs[behind] = jnp.broadcast_to(seg_ref[:, at], (rows, rows))
    key_index = lax.broadcasted_iota(jnp.int32, (rows, rows), 0)
    query_index = lax.broadcasted_iota(jnp.int32, (rows, rows), 1)
    for place, (query_behind, key_behind, parity) in enumerate(pairs):
        valid = docs[key_behind].T == docs[query_behind]
        if key_behind == query_behind:
            valid = valid & (key_index <= query_index)
        valid = valid & (rank >= key_behind)
        if parity is not None:
            valid = valid & (rank % 2 == parity)
        bias_ref[place * rows : (place + 1) * rows, :] = jnp.where(valid, 0.0, MASKED)


def raise_maxima(max_ref, q_ref, key_ref, bias_ref, place, floor_ref=None):
    rows = q_ref.shape[0]
    bias = bias_ref[place * rows : (place + 1) * rows, :]
    for head in range(0, QUERY_HEADS, 2):
        column = head // GROUP
        keys = key_ref[:, column * HEAD_SIZE : (column + 1) * HEAD_SIZE]
        q = [q_ref[:, h * HEAD_SIZE : (h + 1) * HEAD_SIZE] for h in (head, head + 1)]
        logits = lax.dot_general(
            keys, jnp.concatenate(q, axis=0), NT, preferred_element_type=jnp.float32
        )
        for i in range(2):
            at = slice(head + i, head + i + 1)
            largest = jnp.max(logits[:, i * rows : (i + 1) * rows] + bias, axis=0, keepdims=True)
            if floor_ref is not None:
                largest = jnp.maximum(floor_ref[at, :], largest)
            max_ref[at, :] = largest


def store_clipped(clipped_ref, max_ref):
    largest = max_ref[...]
    rows = largest.shape[1]
    groups = [
        jnp.max(largest[c * GROUP : (c + 1) * GROUP, :], axis=0, keepdims=True)
        for c in range(KEY_VALUE_HEADS)
    ]
    spare = KEY_HEAD_LANE - QUERY_HEADS
    padded = jnp.concatenate([largest, largest[:spare], *groups, largest, largest], axis=0)[:rows]
    head_max = jnp.max(padded.T, axis=0, keepdims=True) * SCALE
    clipped = clip_level / jnp.maximum(head_max, clip_level)
    clipped_ref[...] = jnp.broadcast_to(clipped[None], clipped_ref.shape)


def load_kernel(
    shards, pairs, seg_hbm, q_hbm, key_hbm, bias_ref, q_ref, key_ref, seg_ref, sems
):
    copies = [
        pltpu.make_async_copy(source, target, sems.at[i])
        for i, (source, target) in enumerate(
            ((seg_hbm, seg_ref), (key_hbm, key_ref), (q_hbm, q_ref))
        )
    ]
    for copy in copies:
        copy.start()
    copies[0].wait()
    fill_bias(seg_ref, bias_ref, lax.axis_index("seq"), shards, pairs, q_ref.shape[0])
    copies[1].wait()
    copies[2].wait()


def first_kernel(bias_ref, q_ref, key_ref, *refs):
    *partner_ref, max_ref = refs[: len(refs) // 2 + 1]
    raise_maxima(max_ref, q_ref, key_ref, bias_ref, 0)
    if partner_ref:
        raise_maxima(refs[-1], partner_ref[0], key_ref, bias_ref, 4, max_ref)


def next_kernel(place, bias_ref, q_ref, before_ref, key_ref, max_ref, *clipped_refs):
    raise_maxima(max_ref, q_ref, key_ref, bias_ref, place, before_ref)
    for clipped_ref in clipped_refs:
        store_clipped(clipped_ref, max_ref)


def last_paired_kernel(
    bias_ref, q_ref, partner_ref, before_ref, near_ref, key_ref, max_ref, clipped_ref, all_ref
):
    raise_maxima(max_ref, q_ref, key_ref, bias_ref, 2, before_ref)
    all_ref[...] = jnp.maximum(near_ref[...], max_ref[...])

    @pl.when(lax.axis_index("seq") % 2 == 1)
    def _():
        raise_maxima(all_ref, partner_ref, key_ref, bias_ref, 3, all_ref)

    store_clipped(clipped_ref, all_ref)


def mix_kernel(blocks, bias_ref, q_ref, row_max_ref, *refs):
    key_refs, value_refs, out_ref = refs[:blocks], refs[blocks:-1], refs[-1]
    for column in range(KEY_VALUE_HEADS):
        at = slice(column * HEAD_SIZE, (column + 1) * HEAD_SIZE)
        key_block = jnp.concatenate([k[:, at] for k in key_refs], axis=0)
        value_block = jnp.concatenate([v[:, at].T for v in value_refs], axis=1)
        for head in range(column * GROUP, (column + 1) * GROUP):
            here = slice(head * HEAD_SIZE, (head + 1) * HEAD_SIZE)
            logits = lax.dot_general(
                key_block, q_ref[:, here], NT, preferred_element_type=jnp.float32
            )
            largest = row_max_ref[head : head + 1, :] * SCALE_2
            expo = jnp.exp2((logits + bias_ref[: key_block.shape[0], :]) * SCALE_2 - largest)
            share = 1.0 / jnp.sum(expo, axis=0, keepdims=True)
            mixed = jnp.dot(
                value_block, expo.astype(jnp.bfloat16), preferred_element_type=jnp.float32
            )
            out_ref[:, here] = (mixed * share).astype(jnp.bfloat16).T


def mix_paired_kernel(bias_ref, q_ref, row_max_ref, own, near, far, *refs):
    *value_refs, out_ref, max_ref = refs
    raise_maxima(max_ref, q_ref, near, bias_ref, 1, row_max_ref)
    mix_kernel(3, bias_ref, q_ref, max_ref, own, near, far, *value_refs, out_ref)


VMEM = pl.BlockSpec(memory_space=pltpu.VMEM)


def call(kernel, name, out_shape, blocks, products, *arrays, scratch=()):
    rows = out_shape[0].shape[-1] if products == 1 else out_shape[0].shape[0]
    pairs = QUERY_HEADS * rows * rows * blocks
    return pl.pallas_call(
        kernel,
        out_shape=out_shape,
        in_specs=[VMEM] * len(arrays),
        out_specs=(VMEM,) * len(out_shape),
        scratch_shapes=scratch,
        compiler_params=pltpu.CompilerParams(vmem_limit_bytes=24 << 20),
        cost_estimate=pl.CostEstimate(
            flops=2 * products * HEAD_SIZE * pairs,
            bytes_accessed=2 * QUERY_HEADS * HEAD_SIZE * rows * products,
            transcendentals=(products - 1) * pairs,
        ),
        name=name,
    )(*arrays)


def load(shards, pairs, segments, queries, keys):
    rows = queries.shape[0]
    hbm = pl.BlockSpec(memory_space=pltpu.HBM)
    operands = [
        pltpu.with_memory_space_constraint(x, pltpu.HBM) for x in (segments, queries, keys)
    ]
    return pl.pallas_call(
        functools.partial(load_kernel, shards, pairs),
        out_shape=(
            pltpu.VMEM((len(pairs) * rows, rows), jnp.float32),
            pltpu.VMEM(queries.shape, queries.dtype),
            pltpu.VMEM(keys.shape, keys.dtype),
        ),
        in_specs=[hbm] * 3,
        out_specs=(VMEM,) * 3,
        scratch_shapes=[
            pltpu.VMEM(segments.shape, segments.dtype),
            pltpu.SemaphoreType.DMA((3,)),
        ],
        compiler_params=pltpu.CompilerParams(vmem_limit_bytes=24 << 20),
        cost_estimate=pl.CostEstimate(
            flops=0, bytes_accessed=2 * (queries.size + keys.size), transcendentals=0
        ),
        name="load",
    )(*operands)


def in_vmem(x):
    return pltpu.with_memory_space_constraint(x, pltpu.VMEM)


def float32(*shape):
    return jax.ShapeDtypeStruct(shape, jnp.float32)


def like(x):
    return jax.ShapeDtypeStruct(x.shape, x.dtype)


def plan_of_pairs(segments, queries, keys, values, devices):
    rows = queries.shape[0]
    across = [(i, i ^ 2) for i in range(4)]
    swap = [(i, i ^ 1) for i in range(4)]
    rotate = [(i, (i + 1) % 4) for i in range(4)]
    far_keys = lax.ppermute(keys, "seq", across)
    partner_queries = lax.ppermute(queries, "seq", swap)
    pairs = ((0, 0, None), (0, 1, None), (0, 2, None), (1, 2, 1), (-1, 0, 0))
    max_shape = float32(QUERY_HEADS, rows)
    bias, queries, own_keys = load(4, pairs, segments, queries, keys)
    row_max, near_max = call(
        first_kernel,
        "first_maxima",
        (max_shape, max_shape),
        2,
        1,
        bias,
        queries,
        own_keys,
        partner_queries,
    )
    sent_keys, values, near_max = lax.optimization_barrier((keys, values, near_max))
    far_values = lax.ppermute(values, "seq", across)
    near_values = lax.ppermute(values, "seq", rotate)
    near_keys = lax.ppermute(sent_keys, "seq", rotate)
    row_max, clipped = call(
        last_paired_kernel,
        "last_maxima",
        (max_shape, pltpu.VMEM((devices, 1, rows), jnp.float32)),
        2,
        1,
        bias,
        queries,
        partner_queries,
        row_max,
        near_max,
        in_vmem(far_keys),
        scratch=[pltpu.VMEM(max_shape.shape, jnp.float32)],
    )
    everyone = lax.all_to_all(clipped, ("dp", "seq"), 0, 0)
    (attended,) = call(
        mix_paired_kernel,
        "mix",
        (like(queries),),
        3,
        2,
        bias,
        queries,
        row_max,
        own_keys,
        in_vmem(near_keys),
        in_vmem(far_keys),
        in_vmem(values),
        in_vmem(near_values),
        in_vmem(far_values),
        scratch=[pltpu.VMEM(max_shape.shape, jnp.float32)],
    )
    return attended, everyone


def plan_of_rotations(segments, queries, keys, values, devices, reach, shards):
    def passed_along(x, by):
        return lax.ppermute(x, "seq", [(i, (i + by) % shards) for i in range(shards)])

    rows = queries.shape[0]
    distances = range(reach, 0, -1)
    key_blocks = {d: passed_along(keys, d) for d in distances}
    pairs = tuple((0, d, None) for d in range(reach + 1))
    max_shape = float32(QUERY_HEADS, rows)
    bias, queries, own_keys = load(shards, pairs, segments, queries, keys)
    (row_max,) = call(
        first_kernel, "first_maxima", (max_shape,), 1, 1, bias, queries, own_keys
    )
    sent_values, bias = lax.optimization_barrier((values, bias))
    value_blocks = {d: passed_along(sent_values, d) for d in distances}
    for d in distances:
        out_shape = (max_shape,) + ((float32(devices, 1, rows),) if d == 1 else ())
        row_max, *clipped = call(
            functools.partial(next_kernel, d),
            f"maxima_{d}",
            out_shape,
            1,
            1,
            bias,
            queries,
            row_max,
            key_blocks[d],
        )
    everyone = lax.all_to_all(clipped[0], ("dp", "seq"), 0, 0)
    (attended,) = call(
        functools.partial(mix_kernel, reach + 1),
        "mix",
        (like(queries),),
        reach + 1,
        2,
        bias,
        queries,
        row_max,
        own_keys,
        *[key_blocks[d] for d in range(1, reach + 1)],
        values,
        *[value_blocks[d] for d in range(1, reach + 1)],
    )
    return attended, everyone


def clip_factors(clipped, smallest):
    key_head_factor = jnp.sqrt(smallest)
    return (clipped / jnp.repeat(key_head_factor, GROUP), key_head_factor)


def local(queries, keys, values, segments):
    rows, length = queries.shape[1], segments.shape[1]
    shards = lax.axis_size("seq")
    devices = lax.axis_size("dp") * shards
    reach = reach_of(rows, length, shards)
    arrays = (segments, queries[0], keys[0], values[0], devices)
    if shards == 4 and reach == 2:
        attended, everyone = plan_of_pairs(*arrays)
    else:
        attended, everyone = plan_of_rotations(*arrays, reach, shards)
    everyone, attended = lax.optimization_barrier((everyone, attended))
    clipped = jnp.min(everyone[:, 0, :], axis=0)
    query_factor, key_head_factor = clip_factors(
        clipped[:QUERY_HEADS], clipped[KEY_HEAD_LANE : KEY_HEAD_LANE + KEY_VALUE_HEADS]
    )
    return (attended[None], query_factor, key_head_factor)


def solution(mesh):
    in_specs = (P("dp", "seq", None), P("dp", "seq", None), P("dp", "seq", None), P("dp", None))
    out_specs = (P("dp", "seq", None), P(), P())
    return jax.shard_map(local, mesh=mesh, in_specs=in_specs, out_specs=out_specs, check_vma=False)
```

```python
import functools
import math

import jax
import jax.numpy as jnp
from jax import lax
from jax.experimental import pallas as pl
from jax.experimental.pallas import tpu as pltpu
from jax.sharding import PartitionSpec as P

QUERY_HEADS = 48
KEY_VALUE_HEADS = 6
HEAD_SIZE = 128
DOCUMENT_LIMIT = 384
GROUP = QUERY_HEADS // KEY_VALUE_HEADS

clip_level = 6.0
SCALE = HEAD_SIZE ** (-0.5)
SCALE_2 = SCALE * math.log2(math.e)
MASKED = -1e30
KEY_HEAD_LANE = 64
NT = (((1,), (1,)), ((), ()))


def reach_of(rows, length, shards):
    reach = (DOCUMENT_LIMIT - 1 + rows - 1) // rows
    documents = length // 256
    least = length - (documents - 1) * DOCUMENT_LIMIT
    if shards == reach + 1 and documents > 1 and least >= rows:
        reach -= 1
    return reach


def fill_bias(seg_ref, bias_ref, rank, shards, pairs, rows):
    docs = {}
    for behind in sorted({b for pair in pairs for b in pair[:2]}):
        block = jnp.clip(rank - behind, 0, shards - 1)
        at = pl.ds(pl.multiple_of(block * rows, rows), rows)
        docs[behind] = jnp.broadcast_to(seg_ref[:, at], (rows, rows))
    key_index = lax.broadcasted_iota(jnp.int32, (rows, rows), 0)
    query_index = lax.broadcasted_iota(jnp.int32, (rows, rows), 1)
    for place, (query_behind, key_behind, parity) in enumerate(pairs):
        valid = docs[key_behind].T == docs[query_behind]
        if key_behind == query_behind:
            valid = valid & (key_index <= query_index)
        valid = valid & (rank >= key_behind)
        if parity is not None:
            valid = valid & (rank % 2 == parity)
        bias_ref[place * rows : (place + 1) * rows, :] = jnp.where(valid, 0.0, MASKED)


def raise_maxima(max_ref, q_ref, key_ref, bias_ref, place, floor_ref=None):
    rows = q_ref.shape[0]
    bias = bias_ref[place * rows : (place + 1) * rows, :]
    for head in range(0, QUERY_HEADS, 2):
        column = head // GROUP
        keys = key_ref[:, column * HEAD_SIZE : (column + 1) * HEAD_SIZE]
        q = [q_ref[:, h * HEAD_SIZE : (h + 1) * HEAD_SIZE] for h in (head, head + 1)]
        logits = lax.dot_general(
            keys, jnp.concatenate(q, axis=0), NT, preferred_element_type=jnp.float32
        )
        for i in range(2):
            at = slice(head + i, head + i + 1)
            largest = jnp.max(logits[:, i * rows : (i + 1) * rows] + bias, axis=0, keepdims=True)
            if floor_ref is not None:
                largest = jnp.maximum(floor_ref[at, :], largest)
            max_ref[at, :] = largest


def store_clipped(clipped_ref, max_ref):
    largest = max_ref[...]
    rows = largest.shape[1]
    groups = [
        jnp.max(largest[c * GROUP : (c + 1) * GROUP, :], axis=0, keepdims=True)
        for c in range(KEY_VALUE_HEADS)
    ]
    spare = KEY_HEAD_LANE - QUERY_HEADS
    padded = jnp.concatenate([largest, largest[:spare], *groups, largest, largest], axis=0)[:rows]
    head_max = jnp.max(padded.T, axis=0, keepdims=True) * SCALE
    clipped = clip_level / jnp.maximum(head_max, clip_level)
    clipped_ref[...] = jnp.broadcast_to(clipped, clipped_ref.shape)


def load_kernel(
    shards, pairs, seg_hbm, q_hbm, key_hbm, bias_ref, q_ref, key_ref, seg_ref, sems
):
    copies = [
        pltpu.make_async_copy(source, target, sems.at[i])
        for i, (source, target) in enumerate(
            ((seg_hbm, seg_ref), (key_hbm, key_ref), (q_hbm, q_ref))
        )
    ]
    for copy in copies:
        copy.start()
    copies[0].wait()
    fill_bias(seg_ref, bias_ref, lax.axis_index("seq"), shards, pairs, q_ref.shape[0])
    copies[1].wait()
    copies[2].wait()


def first_kernel(bias_ref, q_ref, key_ref, *refs):
    *partner_ref, max_ref = refs[: len(refs) // 2 + 1]
    raise_maxima(max_ref, q_ref, key_ref, bias_ref, 0)
    if partner_ref:
        raise_maxima(refs[-1], partner_ref[0], key_ref, bias_ref, 4, max_ref)


def next_kernel(place, bias_ref, q_ref, before_ref, key_ref, max_ref, *clipped_refs):
    raise_maxima(max_ref, q_ref, key_ref, bias_ref, place, before_ref)
    for clipped_ref in clipped_refs:
        store_clipped(clipped_ref, max_ref)


def last_paired_kernel(
    bias_ref, q_ref, partner_ref, before_ref, near_ref, key_ref, max_ref, clipped_ref, all_ref
):
    raise_maxima(max_ref, q_ref, key_ref, bias_ref, 2, before_ref)
    all_ref[...] = jnp.maximum(near_ref[...], max_ref[...])

    @pl.when(lax.axis_index("seq") % 2 == 1)
    def _():
        raise_maxima(all_ref, partner_ref, key_ref, bias_ref, 3, all_ref)

    store_clipped(clipped_ref, all_ref)


def mix_kernel(blocks, bias_ref, q_ref, row_max_ref, *refs):
    key_refs, value_refs, out_ref = refs[:blocks], refs[blocks:-1], refs[-1]
    for column in range(KEY_VALUE_HEADS):
        at = slice(column * HEAD_SIZE, (column + 1) * HEAD_SIZE)
        key_block = jnp.concatenate([k[:, at] for k in key_refs], axis=0)
        value_block = jnp.concatenate([v[:, at].T for v in value_refs], axis=1)
        for head in range(column * GROUP, (column + 1) * GROUP):
            here = slice(head * HEAD_SIZE, (head + 1) * HEAD_SIZE)
            logits = lax.dot_general(
                key_block, q_ref[:, here], NT, preferred_element_type=jnp.float32
            )
            largest = row_max_ref[head : head + 1, :] * SCALE_2
            expo = jnp.exp2((logits + bias_ref[: key_block.shape[0], :]) * SCALE_2 - largest)
            share = 1.0 / jnp.sum(expo, axis=0, keepdims=True)
            mixed = jnp.dot(
                value_block, expo.astype(jnp.bfloat16), preferred_element_type=jnp.float32
            )
            out_ref[:, here] = (mixed * share).astype(jnp.bfloat16).T


def mix_paired_kernel(bias_ref, q_ref, row_max_ref, own, near, far, *refs):
    *value_refs, out_ref, max_ref = refs
    raise_maxima(max_ref, q_ref, near, bias_ref, 1, row_max_ref)
    mix_kernel(3, bias_ref, q_ref, max_ref, own, near, far, *value_refs, out_ref)


VMEM = pl.BlockSpec(memory_space=pltpu.VMEM)


def call(kernel, name, out_shape, blocks, products, *arrays, scratch=()):
    rows = out_shape[0].shape[-1] if products == 1 else out_shape[0].shape[0]
    pairs = QUERY_HEADS * rows * rows * blocks
    return pl.pallas_call(
        kernel,
        out_shape=out_shape,
        in_specs=[VMEM] * len(arrays),
        out_specs=(VMEM,) * len(out_shape),
        scratch_shapes=scratch,
        compiler_params=pltpu.CompilerParams(vmem_limit_bytes=24 << 20),
        cost_estimate=pl.CostEstimate(
            flops=2 * products * HEAD_SIZE * pairs,
            bytes_accessed=2 * QUERY_HEADS * HEAD_SIZE * rows * products,
            transcendentals=(products - 1) * pairs,
        ),
        name=name,
    )(*arrays)


def load(shards, pairs, segments, queries, keys):
    rows = queries.shape[0]
    hbm = pl.BlockSpec(memory_space=pltpu.HBM)
    operands = [
        pltpu.with_memory_space_constraint(x, pltpu.HBM) for x in (segments, queries, keys)
    ]
    return pl.pallas_call(
        functools.partial(load_kernel, shards, pairs),
        out_shape=(
            pltpu.VMEM((len(pairs) * rows, rows), jnp.float32),
            pltpu.VMEM(queries.shape, queries.dtype),
            pltpu.VMEM(keys.shape, keys.dtype),
        ),
        in_specs=[hbm] * 3,
        out_specs=(VMEM,) * 3,
        scratch_shapes=[
            pltpu.VMEM(segments.shape, segments.dtype),
            pltpu.SemaphoreType.DMA((3,)),
        ],
        compiler_params=pltpu.CompilerParams(vmem_limit_bytes=24 << 20),
        cost_estimate=pl.CostEstimate(
            flops=0, bytes_accessed=2 * (queries.size + keys.size), transcendentals=0
        ),
        name="load",
    )(*operands)


def in_vmem(x):
    return pltpu.with_memory_space_constraint(x, pltpu.VMEM)


def float32(*shape):
    return jax.ShapeDtypeStruct(shape, jnp.float32)


def like(x):
    return jax.ShapeDtypeStruct(x.shape, x.dtype)


def plan_of_pairs(segments, queries, keys, values, devices):
    rows = queries.shape[0]
    across = [(i, i ^ 2) for i in range(4)]
    swap = [(i, i ^ 1) for i in range(4)]
    rotate = [(i, (i + 1) % 4) for i in range(4)]
    far_keys = lax.ppermute(keys, "seq", across)
    partner_queries = lax.ppermute(queries, "seq", swap)
    pairs = ((0, 0, None), (0, 1, None), (0, 2, None), (1, 2, 1), (-1, 0, 0))
    max_shape = float32(QUERY_HEADS, rows)
    bias, queries, own_keys = load(4, pairs, segments, queries, keys)
    row_max, near_max = call(
        first_kernel,
        "first_maxima",
        (max_shape, max_shape),
        2,
        1,
        bias,
        queries,
        own_keys,
        partner_queries,
    )
    sent_keys, values, near_max = lax.optimization_barrier((keys, values, near_max))
    far_values = lax.ppermute(values, "seq", across)
    near_values = lax.ppermute(values, "seq", rotate)
    near_keys = lax.ppermute(sent_keys, "seq", rotate)
    row_max, clipped = call(
        last_paired_kernel,
        "last_maxima",
        (max_shape, float32(devices, rows)),
        2,
        1,
        bias,
        queries,
        partner_queries,
        row_max,
        near_max,
        in_vmem(far_keys),
        scratch=[pltpu.VMEM(max_shape.shape, jnp.float32)],
    )
    everyone = lax.all_to_all(clipped, ("dp", "seq"), 0, 0, tiled=True)
    (attended,) = call(
        mix_paired_kernel,
        "mix",
        (like(queries),),
        3,
        2,
        bias,
        queries,
        row_max,
        own_keys,
        in_vmem(near_keys),
        in_vmem(far_keys),
        in_vmem(values),
        in_vmem(near_values),
        in_vmem(far_values),
        scratch=[pltpu.VMEM(max_shape.shape, jnp.float32)],
    )
    return attended, everyone


def plan_of_rotations(segments, queries, keys, values, devices, reach, shards):
    def passed_along(x, by):
        return lax.ppermute(x, "seq", [(i, (i + by) % shards) for i in range(shards)])

    rows = queries.shape[0]
    distances = range(reach, 0, -1)
    key_blocks = {d: passed_along(keys, d) for d in distances}
    pairs = tuple((0, d, None) for d in range(reach + 1))
    max_shape = float32(QUERY_HEADS, rows)
    bias, queries, own_keys = load(shards, pairs, segments, queries, keys)
    (row_max,) = call(
        first_kernel, "first_maxima", (max_shape,), 1, 1, bias, queries, own_keys
    )
    sent_values, bias = lax.optimization_barrier((values, bias))
    value_blocks = {d: passed_along(sent_values, d) for d in distances}
    for d in distances:
        out_shape = (max_shape,) + ((float32(devices, rows),) if d == 1 else ())
        row_max, *clipped = call(
            functools.partial(next_kernel, d),
            f"maxima_{d}",
            out_shape,
            1,
            1,
            bias,
            queries,
            row_max,
            key_blocks[d],
        )
    everyone = lax.all_to_all(clipped[0], ("dp", "seq"), 0, 0, tiled=True)
    (attended,) = call(
        functools.partial(mix_kernel, reach + 1),
        "mix",
        (like(queries),),
        reach + 1,
        2,
        bias,
        queries,
        row_max,
        own_keys,
        *[key_blocks[d] for d in range(1, reach + 1)],
        values,
        *[value_blocks[d] for d in range(1, reach + 1)],
    )
    return attended, everyone


def clip_factors(clipped, smallest):
    key_head_factor = jnp.sqrt(smallest)
    return (clipped / jnp.repeat(key_head_factor, GROUP), key_head_factor)


def local(queries, keys, values, segments):
    rows, length = queries.shape[1], segments.shape[1]
    shards = lax.axis_size("seq")
    devices = lax.axis_size("dp") * shards
    reach = reach_of(rows, length, shards)
    arrays = (segments, queries[0], keys[0], values[0], devices)
    if shards == 4 and reach == 2:
        attended, everyone = plan_of_pairs(*arrays)
    else:
        attended, everyone = plan_of_rotations(*arrays, reach, shards)
    everyone, attended = lax.optimization_barrier((everyone, attended))
    clipped = jnp.min(everyone, axis=0)
    query_factor, key_head_factor = clip_factors(
        clipped[:QUERY_HEADS], clipped[KEY_HEAD_LANE : KEY_HEAD_LANE + KEY_VALUE_HEADS]
    )
    return (attended[None], query_factor, key_head_factor)


def solution(mesh):
    in_specs = (P("dp", "seq", None), P("dp", "seq", None), P("dp", "seq", None), P("dp", None))
    out_specs = (P("dp", "seq", None), P(), P())
    return jax.shard_map(local, mesh=mesh, in_specs=in_specs, out_specs=out_specs, check_vma=False)
```

```python
import functools
import math

import jax
import jax.numpy as jnp
from jax import lax
from jax.experimental import pallas as pl
from jax.experimental.pallas import tpu as pltpu
from jax.sharding import PartitionSpec as P

QUERY_HEADS = 48
KEY_VALUE_HEADS = 6
HEAD_SIZE = 128
DOCUMENT_LIMIT = 384
GROUP = QUERY_HEADS // KEY_VALUE_HEADS

clip_level = 6.0
SCALE = HEAD_SIZE ** (-0.5)
SCALE_2 = SCALE * math.log2(math.e)
MASKED = -1e30
KEY_HEAD_LANE = 64
WIDE = 4
NT = (((1,), (1,)), ((), ()))


def reach_of(rows, length, shards):
    reach = (DOCUMENT_LIMIT - 1 + rows - 1) // rows
    documents = length // 256
    least = length - (documents - 1) * DOCUMENT_LIMIT
    if shards == reach + 1 and documents > 1 and least >= rows:
        reach -= 1
    return reach


def fill_bias(seg_ref, bias_ref, rank, shards, pairs, rows):
    docs = {}
    for behind in sorted({b for pair in pairs for b in pair[:2]}):
        block = jnp.clip(rank - behind, 0, shards - 1)
        at = pl.ds(pl.multiple_of(block * rows, rows), rows)
        docs[behind] = jnp.broadcast_to(seg_ref[:, at], (rows, rows))
    key_index = lax.broadcasted_iota(jnp.int32, (rows, rows), 0)
    query_index = lax.broadcasted_iota(jnp.int32, (rows, rows), 1)
    for place, (query_behind, key_behind, parity) in enumerate(pairs):
        valid = docs[key_behind].T == docs[query_behind]
        if key_behind == query_behind:
            valid = valid & (key_index <= query_index)
        valid = valid & (rank >= key_behind)
        if parity is not None:
            valid = valid & (rank % 2 == parity)
        bias_ref[place * rows : (place + 1) * rows, :] = jnp.where(valid, 0.0, MASKED)


def raise_maxima(max_ref, q_ref, key_ref, bias_ref, place, floor_ref=None):
    rows = q_ref.shape[0]
    bias = bias_ref[place * rows : (place + 1) * rows, :]
    for head in range(0, QUERY_HEADS, WIDE):
        column = head // GROUP
        keys = key_ref[:, column * HEAD_SIZE : (column + 1) * HEAD_SIZE]
        q = [q_ref[:, h * HEAD_SIZE : (h + 1) * HEAD_SIZE] for h in range(head, head + WIDE)]
        logits = lax.dot_general(
            keys, jnp.concatenate(q, axis=0), NT, preferred_element_type=jnp.float32
        )
        for i in range(WIDE):
            at = slice(head + i, head + i + 1)
            largest = jnp.max(logits[:, i * rows : (i + 1) * rows] + bias, axis=0, keepdims=True)
            if floor_ref is not None:
                largest = jnp.maximum(floor_ref[at, :], largest)
            max_ref[at, :] = largest


def store_clipped(clipped_ref, max_ref):
    largest = max_ref[...]
    rows = largest.shape[1]
    groups = [
        jnp.max(largest[c * GROUP : (c + 1) * GROUP, :], axis=0, keepdims=True)
        for c in range(KEY_VALUE_HEADS)
    ]
    spare = KEY_HEAD_LANE - QUERY_HEADS
    padded = jnp.concatenate([largest, largest[:spare], *groups, largest, largest], axis=0)[:rows]
    head_max = jnp.max(padded.T, axis=0, keepdims=True) * SCALE
    clipped = clip_level / jnp.maximum(head_max, clip_level)
    clipped_ref[...] = jnp.broadcast_to(clipped, clipped_ref.shape)


def load_kernel(
    shards, pairs, seg_hbm, q_hbm, key_hbm, bias_ref, q_ref, key_ref, seg_ref, sems
):
    copies = [
        pltpu.make_async_copy(source, target, sems.at[i])
        for i, (source, target) in enumerate(
            ((seg_hbm, seg_ref), (key_hbm, key_ref), (q_hbm, q_ref))
        )
    ]
    for copy in copies:
        copy.start()
    copies[0].wait()
    fill_bias(seg_ref, bias_ref, lax.axis_index("seq"), shards, pairs, q_ref.shape[0])
    copies[1].wait()
    copies[2].wait()


def first_kernel(bias_ref, q_ref, key_ref, *refs):
    *partner_ref, max_ref = refs[: len(refs) // 2 + 1]
    raise_maxima(max_ref, q_ref, key_ref, bias_ref, 0)
    if partner_ref:
        raise_maxima(refs[-1], partner_ref[0], key_ref, bias_ref, 4, max_ref)


def next_kernel(place, bias_ref, q_ref, before_ref, key_ref, max_ref, *clipped_refs):
    raise_maxima(max_ref, q_ref, key_ref, bias_ref, place, before_ref)
    for clipped_ref in clipped_refs:
        store_clipped(clipped_ref, max_ref)


def last_paired_kernel(
    bias_ref, q_ref, partner_ref, before_ref, near_ref, key_ref, max_ref, clipped_ref, all_ref
):
    raise_maxima(max_ref, q_ref, key_ref, bias_ref, 2, before_ref)
    all_ref[...] = jnp.maximum(near_ref[...], max_ref[...])

    @pl.when(lax.axis_index("seq") % 2 == 1)
    def _():
        raise_maxima(all_ref, partner_ref, key_ref, bias_ref, 3, all_ref)

    store_clipped(clipped_ref, all_ref)


def mix_kernel(blocks, bias_ref, q_ref, row_max_ref, *refs):
    key_refs, value_refs, out_ref = refs[:blocks], refs[blocks:-1], refs[-1]
    for column in range(KEY_VALUE_HEADS):
        at = slice(column * HEAD_SIZE, (column + 1) * HEAD_SIZE)
        key_block = jnp.concatenate([k[:, at] for k in key_refs], axis=0)
        value_block = jnp.concatenate([v[:, at].T for v in value_refs], axis=1)
        for head in range(column * GROUP, (column + 1) * GROUP):
            here = slice(head * HEAD_SIZE, (head + 1) * HEAD_SIZE)
            logits = lax.dot_general(
                key_block, q_ref[:, here], NT, preferred_element_type=jnp.float32
            )
            largest = row_max_ref[head : head + 1, :] * SCALE_2
            expo = jnp.exp2((logits + bias_ref[: key_block.shape[0], :]) * SCALE_2 - largest)
            share = 1.0 / jnp.sum(expo, axis=0, keepdims=True)
            mixed = jnp.dot(
                value_block, expo.astype(jnp.bfloat16), preferred_element_type=jnp.float32
            )
            out_ref[:, here] = (mixed * share).astype(jnp.bfloat16).T


def mix_paired_kernel(bias_ref, q_ref, row_max_ref, own, near, far, *refs):
    *value_refs, out_ref, max_ref = refs
    raise_maxima(max_ref, q_ref, near, bias_ref, 1, row_max_ref)
    mix_kernel(3, bias_ref, q_ref, max_ref, own, near, far, *value_refs, out_ref)


VMEM = pl.BlockSpec(memory_space=pltpu.VMEM)


def call(kernel, name, out_shape, blocks, products, *arrays, scratch=()):
    rows = out_shape[0].shape[-1] if products == 1 else out_shape[0].shape[0]
    pairs = QUERY_HEADS * rows * rows * blocks
    return pl.pallas_call(
        kernel,
        out_shape=out_shape,
        in_specs=[VMEM] * len(arrays),
        out_specs=(VMEM,) * len(out_shape),
        scratch_shapes=scratch,
        compiler_params=pltpu.CompilerParams(vmem_limit_bytes=24 << 20),
        cost_estimate=pl.CostEstimate(
            flops=2 * products * HEAD_SIZE * pairs,
            bytes_accessed=2 * QUERY_HEADS * HEAD_SIZE * rows * products,
            transcendentals=(products - 1) * pairs,
        ),
        name=name,
    )(*arrays)


def load(shards, pairs, segments, queries, keys):
    rows = queries.shape[0]
    hbm = pl.BlockSpec(memory_space=pltpu.HBM)
    operands = [
        pltpu.with_memory_space_constraint(x, pltpu.HBM) for x in (segments, queries, keys)
    ]
    return pl.pallas_call(
        functools.partial(load_kernel, shards, pairs),
        out_shape=(
            pltpu.VMEM((len(pairs) * rows, rows), jnp.float32),
            pltpu.VMEM(queries.shape, queries.dtype),
            pltpu.VMEM(keys.shape, keys.dtype),
        ),
        in_specs=[hbm] * 3,
        out_specs=(VMEM,) * 3,
        scratch_shapes=[
            pltpu.VMEM(segments.shape, segments.dtype),
            pltpu.SemaphoreType.DMA((3,)),
        ],
        compiler_params=pltpu.CompilerParams(vmem_limit_bytes=24 << 20),
        cost_estimate=pl.CostEstimate(
            flops=0, bytes_accessed=2 * (queries.size + keys.size), transcendentals=0
        ),
        name="load",
    )(*operands)


def in_vmem(x):
    return pltpu.with_memory_space_constraint(x, pltpu.VMEM)


def float32(*shape):
    return jax.ShapeDtypeStruct(shape, jnp.float32)


def like(x):
    return jax.ShapeDtypeStruct(x.shape, x.dtype)


def plan_of_pairs(segments, queries, keys, values, devices):
    rows = queries.shape[0]
    across = [(i, i ^ 2) for i in range(4)]
    swap = [(i, i ^ 1) for i in range(4)]
    rotate = [(i, (i + 1) % 4) for i in range(4)]
    far_keys = lax.ppermute(keys, "seq", across)
    partner_queries = lax.ppermute(queries, "seq", swap)
    pairs = ((0, 0, None), (0, 1, None), (0, 2, None), (1, 2, 1), (-1, 0, 0))
    max_shape = float32(QUERY_HEADS, rows)
    bias, queries, own_keys = load(4, pairs, segments, queries, keys)
    row_max, near_max = call(
        first_kernel,
        "first_maxima",
        (max_shape, max_shape),
        2,
        1,
        bias,
        queries,
        own_keys,
        partner_queries,
    )
    sent_keys, values, near_max = lax.optimization_barrier((keys, values, near_max))
    far_values = lax.ppermute(values, "seq", across)
    near_values = lax.ppermute(values, "seq", rotate)
    near_keys = lax.ppermute(sent_keys, "seq", rotate)
    row_max, clipped = call(
        last_paired_kernel,
        "last_maxima",
        (max_shape, float32(devices, rows)),
        2,
        1,
        bias,
        queries,
        partner_queries,
        row_max,
        near_max,
        in_vmem(far_keys),
        scratch=[pltpu.VMEM(max_shape.shape, jnp.float32)],
    )
    everyone = lax.all_to_all(clipped, ("dp", "seq"), 0, 0, tiled=True)
    (attended,) = call(
        mix_paired_kernel,
        "mix",
        (like(queries),),
        3,
        2,
        bias,
        queries,
        row_max,
        own_keys,
        in_vmem(near_keys),
        in_vmem(far_keys),
        in_vmem(values),
        in_vmem(near_values),
        in_vmem(far_values),
        scratch=[pltpu.VMEM(max_shape.shape, jnp.float32)],
    )
    return attended, everyone


def plan_of_rotations(segments, queries, keys, values, devices, reach, shards):
    def passed_along(x, by):
        return lax.ppermute(x, "seq", [(i, (i + by) % shards) for i in range(shards)])

    rows = queries.shape[0]
    distances = range(reach, 0, -1)
    key_blocks = {d: passed_along(keys, d) for d in distances}
    pairs = tuple((0, d, None) for d in range(reach + 1))
    max_shape = float32(QUERY_HEADS, rows)
    bias, queries, own_keys = load(shards, pairs, segments, queries, keys)
    (row_max,) = call(
        first_kernel, "first_maxima", (max_shape,), 1, 1, bias, queries, own_keys
    )
    sent_values, bias = lax.optimization_barrier((values, bias))
    value_blocks = {d: passed_along(sent_values, d) for d in distances}
    for d in distances:
        out_shape = (max_shape,) + ((float32(devices, rows),) if d == 1 else ())
        row_max, *clipped = call(
            functools.partial(next_kernel, d),
            f"maxima_{d}",
            out_shape,
            1,
            1,
            bias,
            queries,
            row_max,
            key_blocks[d],
        )
    everyone = lax.all_to_all(clipped[0], ("dp", "seq"), 0, 0, tiled=True)
    (attended,) = call(
        functools.partial(mix_kernel, reach + 1),
        "mix",
        (like(queries),),
        reach + 1,
        2,
        bias,
        queries,
        row_max,
        own_keys,
        *[key_blocks[d] for d in range(1, reach + 1)],
        values,
        *[value_blocks[d] for d in range(1, reach + 1)],
    )
    return attended, everyone


def clip_factors(clipped, smallest):
    key_head_factor = jnp.sqrt(smallest)
    return (clipped / jnp.repeat(key_head_factor, GROUP), key_head_factor)


def local(queries, keys, values, segments):
    rows, length = queries.shape[1], segments.shape[1]
    shards = lax.axis_size("seq")
    devices = lax.axis_size("dp") * shards
    reach = reach_of(rows, length, shards)
    arrays = (segments, queries[0], keys[0], values[0], devices)
    if shards == 4 and reach == 2:
        attended, everyone = plan_of_pairs(*arrays)
    else:
        attended, everyone = plan_of_rotations(*arrays, reach, shards)
    everyone, attended = lax.optimization_barrier((everyone, attended))
    clipped = jnp.min(everyone, axis=0)
    query_factor, key_head_factor = clip_factors(
        clipped[:QUERY_HEADS], clipped[KEY_HEAD_LANE : KEY_HEAD_LANE + KEY_VALUE_HEADS]
    )
    return (attended[None], query_factor, key_head_factor)


def solution(mesh):
    in_specs = (P("dp", "seq", None), P("dp", "seq", None), P("dp", "seq", None), P("dp", None))
    out_specs = (P("dp", "seq", None), P(), P())
    return jax.shard_map(local, mesh=mesh, in_specs=in_specs, out_specs=out_specs, check_vma=False)
```

```python
import functools
import math

import jax
import jax.numpy as jnp
from jax import lax
from jax.experimental import pallas as pl
from jax.experimental.pallas import tpu as pltpu
from jax.sharding import PartitionSpec as P

QUERY_HEADS = 48
KEY_VALUE_HEADS = 6
HEAD_SIZE = 128
DOCUMENT_LIMIT = 384
GROUP = QUERY_HEADS // KEY_VALUE_HEADS

clip_level = 6.0
SCALE = HEAD_SIZE ** (-0.5)
SCALE_2 = SCALE * math.log2(math.e)
MASKED = -1e30
GROUP_LANE, KEY_HEAD_LANE = 48, 96
NT = (((1,), (1,)), ((), ()))


def reach_of(rows, length, shards):
    reach = (DOCUMENT_LIMIT - 1 + rows - 1) // rows
    documents = length // 256
    least = length - (documents - 1) * DOCUMENT_LIMIT
    if shards == reach + 1 and documents > 1 and least >= rows:
        reach -= 1
    return reach


def fill_bias(seg_ref, bias_ref, rank, shards, pairs, rows):
    docs = {}
    for behind in sorted({b for pair in pairs for b in pair[:2]}):
        block = jnp.clip(rank - behind, 0, shards - 1)
        at = pl.ds(pl.multiple_of(block * rows, rows), rows)
        docs[behind] = jnp.broadcast_to(seg_ref[:, at], (rows, rows))
    key_index = lax.broadcasted_iota(jnp.int32, (rows, rows), 0)
    query_index = lax.broadcasted_iota(jnp.int32, (rows, rows), 1)
    for place, (query_behind, key_behind, parity) in enumerate(pairs):
        valid = docs[key_behind].T == docs[query_behind]
        if key_behind == query_behind:
            valid = valid & (key_index <= query_index)
        valid = valid & (rank >= key_behind)
        if parity is not None:
            valid = valid & (rank % 2 == parity)
        bias_ref[place * rows : (place + 1) * rows, :] = jnp.where(valid, 0.0, MASKED)


def raise_maxima(max_ref, q_ref, key_ref, bias_ref, place, floor_ref=None):
    rows = q_ref.shape[0]
    bias = bias_ref[place * rows : (place + 1) * rows, :]
    for head in range(0, QUERY_HEADS, 2):
        column = head // GROUP
        keys = key_ref[:, column * HEAD_SIZE : (column + 1) * HEAD_SIZE]
        q = [q_ref[:, h * HEAD_SIZE : (h + 1) * HEAD_SIZE] for h in (head, head + 1)]
        logits = lax.dot_general(
            keys, jnp.concatenate(q, axis=0), NT, preferred_element_type=jnp.float32
        )
        for i in range(2):
            at = slice(head + i, head + i + 1)
            largest = jnp.max(logits[:, i * rows : (i + 1) * rows] + bias, axis=0, keepdims=True)
            if floor_ref is not None:
                largest = jnp.maximum(floor_ref[at, :], largest)
            max_ref[at, :] = largest


def store_clipped(clipped_ref, max_ref):
    largest = max_ref[...]
    rows = largest.shape[1]
    groups = [
        jnp.max(largest[c * GROUP : (c + 1) * GROUP, :], axis=0, keepdims=True)
        for c in range(KEY_VALUE_HEADS)
    ]
    repeated = [jnp.broadcast_to(g, (GROUP, rows)) for g in groups]
    padded = jnp.concatenate([largest, *repeated, *groups, largest], axis=0)[:rows]
    head_max = jnp.max(padded.T, axis=0, keepdims=True) * SCALE
    clipped = clip_level / jnp.maximum(head_max, clip_level)
    clipped_ref[...] = jnp.broadcast_to(clipped[None], clipped_ref.shape)


def load_kernel(
    shards, pairs, seg_hbm, q_hbm, key_hbm, bias_ref, q_ref, key_ref, seg_ref, sems
):
    copies = [
        pltpu.make_async_copy(source, target, sems.at[i])
        for i, (source, target) in enumerate(
            ((seg_hbm, seg_ref), (key_hbm, key_ref), (q_hbm, q_ref))
        )
    ]
    for copy in copies:
        copy.start()
    copies[0].wait()
    fill_bias(seg_ref, bias_ref, lax.axis_index("seq"), shards, pairs, q_ref.shape[0])
    copies[1].wait()
    copies[2].wait()


def first_kernel(bias_ref, q_ref, key_ref, *refs):
    *partner_ref, max_ref = refs[: len(refs) // 2 + 1]
    raise_maxima(max_ref, q_ref, key_ref, bias_ref, 0)
    if partner_ref:
        raise_maxima(refs[-1], partner_ref[0], key_ref, bias_ref, 4, max_ref)


def next_kernel(place, bias_ref, q_ref, before_ref, key_ref, max_ref, *clipped_refs):
    raise_maxima(max_ref, q_ref, key_ref, bias_ref, place, before_ref)
    for clipped_ref in clipped_refs:
        store_clipped(clipped_ref, max_ref)


def last_paired_kernel(
    bias_ref, q_ref, partner_ref, before_ref, near_ref, key_ref, max_ref, clipped_ref, all_ref
):
    raise_maxima(max_ref, q_ref, key_ref, bias_ref, 2, before_ref)
    all_ref[...] = jnp.maximum(near_ref[...], max_ref[...])

    @pl.when(lax.axis_index("seq") % 2 == 1)
    def _():
        raise_maxima(all_ref, partner_ref, key_ref, bias_ref, 3, all_ref)

    store_clipped(clipped_ref, all_ref)


def mix_kernel(blocks, bias_ref, q_ref, row_max_ref, *refs):
    key_refs, value_refs, out_ref = refs[:blocks], refs[blocks:-1], refs[-1]
    for column in range(KEY_VALUE_HEADS):
        at = slice(column * HEAD_SIZE, (column + 1) * HEAD_SIZE)
        key_block = jnp.concatenate([k[:, at] for k in key_refs], axis=0)
        value_block = jnp.concatenate([v[:, at].T for v in value_refs], axis=1)
        for head in range(column * GROUP, (column + 1) * GROUP):
            here = slice(head * HEAD_SIZE, (head + 1) * HEAD_SIZE)
            logits = lax.dot_general(
                key_block, q_ref[:, here], NT, preferred_element_type=jnp.float32
            )
            largest = row_max_ref[head : head + 1, :] * SCALE_2
            expo = jnp.exp2((logits + bias_ref[: key_block.shape[0], :]) * SCALE_2 - largest)
            share = 1.0 / jnp.sum(expo, axis=0, keepdims=True)
            mixed = jnp.dot(
                value_block, expo.astype(jnp.bfloat16), preferred_element_type=jnp.float32
            )
            out_ref[:, here] = (mixed * share).astype(jnp.bfloat16).T


def mix_paired_kernel(bias_ref, q_ref, row_max_ref, own, near, far, *refs):
    *value_refs, out_ref, max_ref = refs
    raise_maxima(max_ref, q_ref, near, bias_ref, 1, row_max_ref)
    mix_kernel(3, bias_ref, q_ref, max_ref, own, near, far, *value_refs, out_ref)


VMEM = pl.BlockSpec(memory_space=pltpu.VMEM)


def call(kernel, name, out_shape, blocks, products, *arrays, scratch=()):
    rows = out_shape[0].shape[-1] if products == 1 else out_shape[0].shape[0]
    pairs = QUERY_HEADS * rows * rows * blocks
    return pl.pallas_call(
        kernel,
        out_shape=out_shape,
        in_specs=[VMEM] * len(arrays),
        out_specs=(VMEM,) * len(out_shape),
        scratch_shapes=scratch,
        compiler_params=pltpu.CompilerParams(vmem_limit_bytes=24 << 20),
        cost_estimate=pl.CostEstimate(
            flops=2 * products * HEAD_SIZE * pairs,
            bytes_accessed=2 * QUERY_HEADS * HEAD_SIZE * rows * products,
            transcendentals=(products - 1) * pairs,
        ),
        name=name,
    )(*arrays)


def load(shards, pairs, segments, queries, keys):
    rows = queries.shape[0]
    hbm = pl.BlockSpec(memory_space=pltpu.HBM)
    operands = [
        pltpu.with_memory_space_constraint(x, pltpu.HBM) for x in (segments, queries, keys)
    ]
    return pl.pallas_call(
        functools.partial(load_kernel, shards, pairs),
        out_shape=(
            pltpu.VMEM((len(pairs) * rows, rows), jnp.float32),
            pltpu.VMEM(queries.shape, queries.dtype),
            pltpu.VMEM(keys.shape, keys.dtype),
        ),
        in_specs=[hbm] * 3,
        out_specs=(VMEM,) * 3,
        scratch_shapes=[
            pltpu.VMEM(segments.shape, segments.dtype),
            pltpu.SemaphoreType.DMA((3,)),
        ],
        compiler_params=pltpu.CompilerParams(vmem_limit_bytes=24 << 20),
        cost_estimate=pl.CostEstimate(
            flops=0, bytes_accessed=2 * (queries.size + keys.size), transcendentals=0
        ),
        name="load",
    )(*operands)


def in_vmem(x):
    return pltpu.with_memory_space_constraint(x, pltpu.VMEM)


def float32(*shape):
    return jax.ShapeDtypeStruct(shape, jnp.float32)


def like(x):
    return jax.ShapeDtypeStruct(x.shape, x.dtype)


def plan_of_pairs(segments, queries, keys, values, devices):
    rows = queries.shape[0]
    across = [(i, i ^ 2) for i in range(4)]
    swap = [(i, i ^ 1) for i in range(4)]
    rotate = [(i, (i + 1) % 4) for i in range(4)]
    far_keys = lax.ppermute(keys, "seq", across)
    partner_queries = lax.ppermute(queries, "seq", swap)
    pairs = ((0, 0, None), (0, 1, None), (0, 2, None), (1, 2, 1), (-1, 0, 0))
    max_shape = float32(QUERY_HEADS, rows)
    bias, queries, own_keys = load(4, pairs, segments, queries, keys)
    row_max, near_max = call(
        first_kernel,
        "first_maxima",
        (max_shape, max_shape),
        2,
        1,
        bias,
        queries,
        own_keys,
        partner_queries,
    )
    sent_keys, values, near_max = lax.optimization_barrier((keys, values, near_max))
    far_values = lax.ppermute(values, "seq", across)
    near_values = lax.ppermute(values, "seq", rotate)
    near_keys = lax.ppermute(sent_keys, "seq", rotate)
    row_max, clipped = call(
        last_paired_kernel,
        "last_maxima",
        (max_shape, pltpu.VMEM((devices, 1, rows), jnp.float32)),
        2,
        1,
        bias,
        queries,
        partner_queries,
        row_max,
        near_max,
        in_vmem(far_keys),
        scratch=[pltpu.VMEM(max_shape.shape, jnp.float32)],
    )
    everyone = lax.all_to_all(clipped, ("dp", "seq"), 0, 0)
    (attended,) = call(
        mix_paired_kernel,
        "mix",
        (like(queries),),
        3,
        2,
        bias,
        queries,
        row_max,
        own_keys,
        in_vmem(near_keys),
        in_vmem(far_keys),
        in_vmem(values),
        in_vmem(near_values),
        in_vmem(far_values),
        scratch=[pltpu.VMEM(max_shape.shape, jnp.float32)],
    )
    return attended, everyone


def plan_of_rotations(segments, queries, keys, values, devices, reach, shards):
    def passed_along(x, by):
        return lax.ppermute(x, "seq", [(i, (i + by) % shards) for i in range(shards)])

    rows = queries.shape[0]
    distances = range(reach, 0, -1)
    key_blocks = {d: passed_along(keys, d) for d in distances}
    pairs = tuple((0, d, None) for d in range(reach + 1))
    max_shape = float32(QUERY_HEADS, rows)
    bias, queries, own_keys = load(shards, pairs, segments, queries, keys)
    (row_max,) = call(
        first_kernel, "first_maxima", (max_shape,), 1, 1, bias, queries, own_keys
    )
    sent_values, bias = lax.optimization_barrier((values, bias))
    value_blocks = {d: passed_along(sent_values, d) for d in distances}
    for d in distances:
        out_shape = (max_shape,) + ((float32(devices, 1, rows),) if d == 1 else ())
        row_max, *clipped = call(
            functools.partial(next_kernel, d),
            f"maxima_{d}",
            out_shape,
            1,
            1,
            bias,
            queries,
            row_max,
            key_blocks[d],
        )
    everyone = lax.all_to_all(clipped[0], ("dp", "seq"), 0, 0)
    (attended,) = call(
        functools.partial(mix_kernel, reach + 1),
        "mix",
        (like(queries),),
        reach + 1,
        2,
        bias,
        queries,
        row_max,
        own_keys,
        *[key_blocks[d] for d in range(1, reach + 1)],
        values,
        *[value_blocks[d] for d in range(1, reach + 1)],
    )
    return attended, everyone


def local(queries, keys, values, segments):
    rows, length = queries.shape[1], segments.shape[1]
    shards = lax.axis_size("seq")
    devices = lax.axis_size("dp") * shards
    reach = reach_of(rows, length, shards)
    arrays = (segments, queries[0], keys[0], values[0], devices)
    if shards == 4 and reach == 2:
        attended, everyone = plan_of_pairs(*arrays)
    else:
        attended, everyone = plan_of_rotations(*arrays, reach, shards)
    everyone, attended = lax.optimization_barrier((everyone, attended))
    clipped = jnp.min(everyone[:, 0, :], axis=0)
    key_head_factor = jnp.sqrt(clipped[KEY_HEAD_LANE : KEY_HEAD_LANE + KEY_VALUE_HEADS])
    smallest = clipped[GROUP_LANE : GROUP_LANE + QUERY_HEADS]
    floor = key_head_factor[0] * 0.0
    query_factor = clipped[:QUERY_HEADS] / jnp.maximum(jnp.sqrt(smallest), floor)
    return (attended[None], query_factor, key_head_factor)


def solution(mesh):
    in_specs = (P("dp", "seq", None), P("dp", "seq", None), P("dp", "seq", None), P("dp", None))
    out_specs = (P("dp", "seq", None), P(), P())
    return jax.shard_map(local, mesh=mesh, in_specs=in_specs, out_specs=out_specs, check_vma=False)
```

```python
import functools
import math

import jax
import jax.numpy as jnp
from jax import lax
from jax.experimental import pallas as pl
from jax.experimental.pallas import tpu as pltpu
from jax.sharding import PartitionSpec as P

QUERY_HEADS = 48
KEY_VALUE_HEADS = 6
HEAD_SIZE = 128
DOCUMENT_LIMIT = 384
GROUP = QUERY_HEADS // KEY_VALUE_HEADS

clip_level = 6.0
SCALE = HEAD_SIZE ** (-0.5)
SCALE_2 = SCALE * math.log2(math.e)
MASKED = -1e30
KEY_HEAD_LANE = 64
NT = (((1,), (1,)), ((), ()))


def reach_of(rows, length, shards):
    reach = (DOCUMENT_LIMIT - 1 + rows - 1) // rows
    documents = length // 256
    least = length - (documents - 1) * DOCUMENT_LIMIT
    if shards == reach + 1 and documents > 1 and least >= rows:
        reach -= 1
    return reach


def fill_bias(seg_ref, bias_ref, rank, shards, pairs, rows):
    docs = {}
    for behind in sorted({b for pair in pairs for b in pair[:2]}):
        block = jnp.clip(rank - behind, 0, shards - 1)
        at = pl.ds(pl.multiple_of(block * rows, rows), rows)
        docs[behind] = jnp.broadcast_to(seg_ref[:, at], (rows, rows))
    key_index = lax.broadcasted_iota(jnp.int32, (rows, rows), 0)
    query_index = lax.broadcasted_iota(jnp.int32, (rows, rows), 1)
    for place, (query_behind, key_behind, parity) in enumerate(pairs):
        valid = docs[key_behind].T == docs[query_behind]
        if key_behind == query_behind:
            valid = valid & (key_index <= query_index)
        valid = valid & (rank >= key_behind)
        if parity is not None:
            valid = valid & (rank % 2 == parity)
        bias_ref[place * rows : (place + 1) * rows, :] = jnp.where(valid, 0.0, MASKED)


def raise_maxima(max_ref, q_ref, key_ref, bias_ref, place, floor_ref=None):
    rows = q_ref.shape[0]
    bias = bias_ref[place * rows : (place + 1) * rows, :]
    for head in range(0, QUERY_HEADS, 2):
        column = head // GROUP
        keys = key_ref[:, column * HEAD_SIZE : (column + 1) * HEAD_SIZE]
        q = [q_ref[:, h * HEAD_SIZE : (h + 1) * HEAD_SIZE] for h in (head, head + 1)]
        logits = lax.dot_general(
            keys, jnp.concatenate(q, axis=0), NT, preferred_element_type=jnp.float32
        )
        for i in range(2):
            at = slice(head + i, head + i + 1)
            largest = jnp.max(logits[:, i * rows : (i + 1) * rows] + bias, axis=0, keepdims=True)
            if floor_ref is not None:
                largest = jnp.maximum(floor_ref[at, :], largest)
            max_ref[at, :] = largest


def store_clipped(clipped_ref, max_ref):
    largest = max_ref[...]
    rows = largest.shape[1]
    groups = [
        jnp.max(largest[c * GROUP : (c + 1) * GROUP, :], axis=0, keepdims=True)
        for c in range(KEY_VALUE_HEADS)
    ]
    spare = KEY_HEAD_LANE - QUERY_HEADS
    padded = jnp.concatenate([largest, largest[:spare], *groups, largest, largest], axis=0)[:rows]
    head_max = jnp.max(padded.T, axis=0, keepdims=True) * SCALE
    clipped = clip_level / jnp.maximum(head_max, clip_level)
    clipped_ref[...] = jnp.broadcast_to(clipped[None], clipped_ref.shape)


def load_kernel(
    shards, pairs, seg_hbm, q_hbm, key_hbm, bias_ref, q_ref, key_ref, seg_ref, sems
):
    copies = [
        pltpu.make_async_copy(source, target, sems.at[i])
        for i, (source, target) in enumerate(
            ((seg_hbm, seg_ref), (key_hbm, key_ref), (q_hbm, q_ref))
        )
    ]
    for copy in copies:
        copy.start()
    copies[0].wait()
    fill_bias(seg_ref, bias_ref, lax.axis_index("seq"), shards, pairs, q_ref.shape[0])
    copies[1].wait()
    copies[2].wait()


def first_kernel(bias_ref, q_ref, key_ref, *refs):
    *partner_ref, max_ref = refs[: len(refs) // 2 + 1]
    raise_maxima(max_ref, q_ref, key_ref, bias_ref, 0)
    if partner_ref:
        raise_maxima(refs[-1], partner_ref[0], key_ref, bias_ref, 4, max_ref)


def next_kernel(place, bias_ref, q_ref, before_ref, key_ref, max_ref, *clipped_refs):
    raise_maxima(max_ref, q_ref, key_ref, bias_ref, place, before_ref)
    for clipped_ref in clipped_refs:
        store_clipped(clipped_ref, max_ref)


def last_paired_kernel(
    bias_ref, q_ref, partner_ref, before_ref, near_ref, key_ref, max_ref, clipped_ref, all_ref
):
    raise_maxima(max_ref, q_ref, key_ref, bias_ref, 2, before_ref)
    all_ref[...] = jnp.maximum(near_ref[...], max_ref[...])

    @pl.when(lax.axis_index("seq") % 2 == 1)
    def _():
        raise_maxima(all_ref, partner_ref, key_ref, bias_ref, 3, all_ref)

    store_clipped(clipped_ref, all_ref)


def mix_kernel(blocks, bias_ref, q_ref, row_max_ref, *refs):
    key_refs, value_refs, out_ref = refs[:blocks], refs[blocks:-1], refs[-1]
    for column in range(KEY_VALUE_HEADS):
        at = slice(column * HEAD_SIZE, (column + 1) * HEAD_SIZE)
        key_block = jnp.concatenate([k[:, at] for k in key_refs], axis=0)
        value_block = jnp.concatenate([v[:, at].T for v in value_refs], axis=1)
        for head in range(column * GROUP, (column + 1) * GROUP):
            here = slice(head * HEAD_SIZE, (head + 1) * HEAD_SIZE)
            logits = lax.dot_general(
                key_block, q_ref[:, here], NT, preferred_element_type=jnp.float32
            )
            largest = row_max_ref[head : head + 1, :] * SCALE_2
            expo = jnp.exp2((logits + bias_ref[: key_block.shape[0], :]) * SCALE_2 - largest)
            share = 1.0 / jnp.sum(expo, axis=0, keepdims=True)
            mixed = jnp.dot(
                value_block, expo.astype(jnp.bfloat16), preferred_element_type=jnp.float32
            )
            out_ref[:, here] = (mixed * share).astype(jnp.bfloat16).T


def mix_paired_kernel(bias_ref, q_ref, row_max_ref, own, near, far, *refs):
    *value_refs, out_ref, max_ref = refs
    raise_maxima(max_ref, q_ref, near, bias_ref, 1, row_max_ref)
    mix_kernel(3, bias_ref, q_ref, max_ref, own, near, far, *value_refs, out_ref)


VMEM = pl.BlockSpec(memory_space=pltpu.VMEM)


def call(kernel, name, out_shape, blocks, products, *arrays, scratch=()):
    rows = out_shape[0].shape[-1] if products == 1 else out_shape[0].shape[0]
    pairs = QUERY_HEADS * rows * rows * blocks
    return pl.pallas_call(
        kernel,
        out_shape=out_shape,
        in_specs=[VMEM] * len(arrays),
        out_specs=(VMEM,) * len(out_shape),
        scratch_shapes=scratch,
        compiler_params=pltpu.CompilerParams(vmem_limit_bytes=24 << 20),
        cost_estimate=pl.CostEstimate(
            flops=2 * products * HEAD_SIZE * pairs,
            bytes_accessed=2 * QUERY_HEADS * HEAD_SIZE * rows * products,
            transcendentals=(products - 1) * pairs,
        ),
        name=name,
    )(*arrays)


def load(shards, pairs, segments, queries, keys):
    rows = queries.shape[0]
    hbm = pl.BlockSpec(memory_space=pltpu.HBM)
    operands = [
        pltpu.with_memory_space_constraint(x, pltpu.HBM) for x in (segments, queries, keys)
    ]
    return pl.pallas_call(
        functools.partial(load_kernel, shards, pairs),
        out_shape=(
            pltpu.VMEM((len(pairs) * rows, rows), jnp.float32),
            pltpu.VMEM(queries.shape, queries.dtype),
            pltpu.VMEM(keys.shape, keys.dtype),
        ),
        in_specs=[hbm] * 3,
        out_specs=(VMEM,) * 3,
        scratch_shapes=[
            pltpu.VMEM(segments.shape, segments.dtype),
            pltpu.SemaphoreType.DMA((3,)),
        ],
        compiler_params=pltpu.CompilerParams(vmem_limit_bytes=24 << 20),
        cost_estimate=pl.CostEstimate(
            flops=0, bytes_accessed=2 * (queries.size + keys.size), transcendentals=0
        ),
        name="load",
    )(*operands)


def in_vmem(x):
    return pltpu.with_memory_space_constraint(x, pltpu.VMEM)


def float32(*shape):
    return jax.ShapeDtypeStruct(shape, jnp.float32)


def like(x):
    return jax.ShapeDtypeStruct(x.shape, x.dtype)


def plan_of_pairs(segments, queries, keys, values, devices):
    rows = queries.shape[0]
    across = [(i, i ^ 2) for i in range(4)]
    swap = [(i, i ^ 1) for i in range(4)]
    rotate = [(i, (i + 1) % 4) for i in range(4)]
    far_keys = lax.ppermute(keys, "seq", across)
    partner_queries = lax.ppermute(queries, "seq", swap)
    pairs = ((0, 0, None), (0, 1, None), (0, 2, None), (1, 2, 1), (-1, 0, 0))
    max_shape = float32(QUERY_HEADS, rows)
    bias, queries, own_keys = load(4, pairs, segments, queries, keys)
    row_max, near_max = call(
        first_kernel,
        "first_maxima",
        (max_shape, max_shape),
        2,
        1,
        bias,
        queries,
        own_keys,
        partner_queries,
    )
    sent_keys, values, near_max = lax.optimization_barrier((keys, values, near_max))
    near_keys = lax.ppermute(sent_keys, "seq", rotate)
    near_values = lax.ppermute(values, "seq", rotate)
    values, near_max = lax.optimization_barrier((values, near_max))
    far_values = lax.ppermute(values, "seq", across)
    row_max, clipped = call(
        last_paired_kernel,
        "last_maxima",
        (max_shape, pltpu.VMEM((devices, 1, rows), jnp.float32)),
        2,
        1,
        bias,
        queries,
        partner_queries,
        row_max,
        near_max,
        in_vmem(far_keys),
        scratch=[pltpu.VMEM(max_shape.shape, jnp.float32)],
    )
    everyone = lax.all_to_all(clipped, ("dp", "seq"), 0, 0)
    (attended,) = call(
        mix_paired_kernel,
        "mix",
        (like(queries),),
        3,
        2,
        bias,
        queries,
        row_max,
        own_keys,
        in_vmem(near_keys),
        in_vmem(far_keys),
        in_vmem(values),
        in_vmem(near_values),
        in_vmem(far_values),
        scratch=[pltpu.VMEM(max_shape.shape, jnp.float32)],
    )
    return attended, everyone


def plan_of_rotations(segments, queries, keys, values, devices, reach, shards):
    def passed_along(x, by):
        return lax.ppermute(x, "seq", [(i, (i + by) % shards) for i in range(shards)])

    rows = queries.shape[0]
    distances = range(reach, 0, -1)
    key_blocks = {d: passed_along(keys, d) for d in distances}
    pairs = tuple((0, d, None) for d in range(reach + 1))
    max_shape = float32(QUERY_HEADS, rows)
    bias, queries, own_keys = load(shards, pairs, segments, queries, keys)
    (row_max,) = call(
        first_kernel, "first_maxima", (max_shape,), 1, 1, bias, queries, own_keys
    )
    sent_values, bias = lax.optimization_barrier((values, bias))
    value_blocks = {d: passed_along(sent_values, d) for d in distances}
    for d in distances:
        out_shape = (max_shape,) + ((float32(devices, 1, rows),) if d == 1 else ())
        row_max, *clipped = call(
            functools.partial(next_kernel, d),
            f"maxima_{d}",
            out_shape,
            1,
            1,
            bias,
            queries,
            row_max,
            key_blocks[d],
        )
    everyone = lax.all_to_all(clipped[0], ("dp", "seq"), 0, 0)
    (attended,) = call(
        functools.partial(mix_kernel, reach + 1),
        "mix",
        (like(queries),),
        reach + 1,
        2,
        bias,
        queries,
        row_max,
        own_keys,
        *[key_blocks[d] for d in range(1, reach + 1)],
        values,
        *[value_blocks[d] for d in range(1, reach + 1)],
    )
    return attended, everyone


def clip_factors(clipped, smallest):
    key_head_factor = jnp.sqrt(smallest)
    return (clipped / jnp.repeat(key_head_factor, GROUP), key_head_factor)


def local(queries, keys, values, segments):
    rows, length = queries.shape[1], segments.shape[1]
    shards = lax.axis_size("seq")
    devices = lax.axis_size("dp") * shards
    reach = reach_of(rows, length, shards)
    arrays = (segments, queries[0], keys[0], values[0], devices)
    if shards == 4 and reach == 2:
        attended, everyone = plan_of_pairs(*arrays)
    else:
        attended, everyone = plan_of_rotations(*arrays, reach, shards)
    everyone, attended = lax.optimization_barrier((everyone, attended))
    clipped = jnp.min(everyone[:, 0, :], axis=0)
    query_factor, key_head_factor = clip_factors(
        clipped[:QUERY_HEADS], clipped[KEY_HEAD_LANE : KEY_HEAD_LANE + KEY_VALUE_HEADS]
    )
    return (attended[None], query_factor, key_head_factor)


def solution(mesh):
    in_specs = (P("dp", "seq", None), P("dp", "seq", None), P("dp", "seq", None), P("dp", None))
    out_specs = (P("dp", "seq", None), P(), P())
    return jax.shard_map(local, mesh=mesh, in_specs=in_specs, out_specs=out_specs, check_vma=False)
```
